512 devices in a mesh: fsdp: 32 (over z_hi, y), tensor: 16 (over z_lo, x, core).
Axes of the slice: x: 4, y: 8, z: 8 (z_hi: 4, z_lo: 2; z = z_hi * 2 + z_lo), core: 2. Of those that a mesh axis runs over, the one named last changes fastest.
Arguments:
- stream_in: bfloat16 [4096, 4096], P('fsdp', 'tensor'), may hold values from -6 to 6
- newer_partial: bfloat16 [16, 4096, 4096], P('tensor', 'fsdp'), may hold values from -1.5 to 1.5
- norm_gain: bfloat16 [4096], replicated, may hold values from 0.099609375 to 1.8984375
- query_weight: bfloat16 [4096, 4096], P('fsdp', 'tensor'), may hold values from -0.09375 to 0.09375
- keys_values: bfloat16 [4096, 2048], P('fsdp'), may hold values from -160 to 160, as said below
- out_weight: bfloat16 [4096, 4096], P('tensor', 'fsdp'), may hold values from -0.09375 to 0.09375
- cot_stream: bfloat16 [4096, 4096], P('fsdp', 'tensor'), may hold values from -0.59765625 to 0.59765625
- cot_attn: bfloat16 [4096, 4096], P('fsdp', 'tensor'), may hold values from -6 to 6
Outputs:
- stream_out: bfloat16 [4096, 4096], P('fsdp')
- attn_partial: bfloat16 [16, 4096, 4096], P('tensor', 'fsdp')
- stream_grad: bfloat16 [4096, 4096], P('fsdp', 'tensor')
- kv_grad: bfloat16 [4096, 2048], P('fsdp')
- query_weight_grad: bfloat16 [4096, 4096], P('fsdp', 'tensor')
- out_weight_grad: bfloat16 [4096, 4096], P('tensor', 'fsdp')
The draws below stay inside these ranges and needn't reach their ends.
Inputs may be any that keep to these rules, and one draw needn't show every extreme that they name: `keys_values`: keys and values of 8 heads, each head's key before its value.
All inputs are finite; a program needn't handle non-finite values.
Results may differ from the reference program's by a relative error of at most 0.035.
The reference program's roundings to bfloat16 on the way (of `normed`, `queries`, `probs_low`, `attended`, `grad_heads`, `grad_scores` and `grad_q`) count: a program that leaves them out, or rounds other values in their place, can miss the bound.
Values may be sent and summed in bfloat16 or wider, within the bound.
No kernel may reach another device: no remote copies, remote signals or barrier semaphores. Data moves between devices by JAX's collectives and lax.ppermute only.
A program may use at most 64 MiB of HBM per device.

```python
import jax
import jax.numpy as jnp
from jax import lax

D = 4096
HEADS = 32
HS = 128
KVH = 8
SEQ = 128
QW = 4096
KVW = 2048
TOKENS = 4096
N_FSDP = 32
N_TENSOR = 16


def draw_keys_values(key, part):
    key = jax.random.fold_in(key, 7)
    first = jax.random.fold_in(key, 0)
    values = jnp.clip(jax.random.normal(first, (TOKENS, KVW), jnp.float32), -4.0, 4.0)
    return values.astype(jnp.bfloat16)


def with_spikes(entries, key, source, target, parts, factor):
    owner, partner = [(jnp.arange(entries.shape[axis_at]) // (entries.shape[axis_at] // parts)).reshape([-1 if axis == axis_at else 1 for axis in range(entries.ndim)]) for axis_at in (source, target)]
    chosen = jax.random.permutation(key, parts)[partner]
    strong = (owner == chosen) | (owner == (partner + parts // 2) % parts)
    return jnp.where(strong, factor * entries, entries)


def block_scale(key, shape, cuts, smallest, high):
    def one(position, shards_of):
        steps = jax.random.uniform(jax.random.fold_in(jax.random.fold_in(key, 6), position), (shards_of,), jnp.float32, smallest / len(cuts), high / len(cuts))
        return jnp.repeat(jnp.exp(steps), shape[position] // shards_of).reshape((-1,) + (1,) * (len(shape) - position - 1))

    factor_of = one(*cuts[0])
    for cut in cuts[1:]:
        factor_of = factor_of * one(*cut)
    return factor_of


def gaussian(rng, dims, scale, bound, shards=(), held_as=jnp.bfloat16):
    values = scale * jax.random.normal(rng, dims, jnp.float32)
    if shards:
        values = values * block_scale(rng, dims, shards, -0.22, 0.18)
    return jnp.clip(values, -bound, bound).astype(held_as)


def gaussian_with(rng, dims, width, limit, cuts, heavy, kind=jnp.bfloat16):
    drawn = width * jax.random.normal(rng, dims, jnp.float32)
    if cuts:
        drawn = drawn * block_scale(rng, dims, cuts, -0.22, 0.18)
    return jnp.clip(with_spikes(drawn, jax.random.fold_in(rng, 3), *heavy), -limit, limit).astype(kind)


def setup_inputs(seed: int = 0) -> dict:
    splits = jax.random.split(jax.random.key(seed), 9)
    return {
        "stream_in": gaussian(splits[0], (TOKENS, D), 1.0, 6.0, ((0, 32), (1, 16))),
        "newer_partial": gaussian(splits[1], (N_TENSOR, TOKENS, D), 0.25, 1.5, ((0, 16), (1, 32))),
        "norm_gain": jnp.clip(1.0 + 0.18 * jax.random.normal(splits[2], (D,), jnp.float32), 0.099609375, 1.8984375).astype(jnp.bfloat16),
        "query_weight": gaussian(splits[3], (D, QW), D ** -0.5, 0.09375, ((0, 32), (1, 16))),
        "keys_values": draw_keys_values(jax.random.fold_in(splits[8], 71), 0),
        "out_weight": gaussian(splits[5], (QW, D), QW ** -0.5, 0.09375, ((0, 16), (1, 32))),
        "cot_stream": gaussian(splits[6], (TOKENS, D), 0.1, 0.59765625, ((0, 32), (1, 16))),
        "cot_attn": gaussian_with(splits[7], (TOKENS, D), 1.0, 6.0, ((0, 32), (1, 16)), (0, 1, 32, 2.75)),
    }


def reference(stream_in, newer_partial, norm_gain, query_weight, keys_values, out_weight, cot_stream, cot_attn):
    heads_here = HEADS // N_TENSOR
    group = HEADS // KVH
    cols = QW // N_TENSOR
    scale = 1.0 / HS ** 0.5

    def add_partial(total, piece):
        return (total + piece.astype(jnp.float32), 0)
    pending, _ = lax.scan(add_partial, jnp.zeros((TOKENS, D), jnp.float32), newer_partial)
    stream_out = (stream_in.astype(jnp.float32) + pending).astype(jnp.bfloat16)
    gain_f = norm_gain.astype(jnp.float32)
    dev_ind = (jnp.arange(HEADS)[:, None] // heads_here == jnp.arange(N_TENSOR)[None, :]).astype(jnp.float32)
    kv_ind = (jnp.arange(HEADS)[:, None] // group == jnp.arange(KVH)[None, :]).astype(jnp.float32)
    causal = jnp.arange(SEQ)[:, None] >= jnp.arange(SEQ)[None, :]
    query_f = query_weight.astype(jnp.float32).reshape(D, N_TENSOR, cols)
    out_f = out_weight.astype(jnp.float32).reshape(N_TENSOR, cols, D)

    def one_sequence(carry, items):
        acc_query, acc_out = carry
        stream, kv, cot_s, cot_a = items
        stream_f = stream.astype(jnp.float32)
        inv_rms = lax.rsqrt(lax.optimization_barrier(jnp.mean(stream_f * stream_f, -1, keepdims=True)) + 1e-05)
        normed = (stream_f * inv_rms * gain_f).astype(jnp.bfloat16)
        queries = jnp.dot(normed, query_weight, preferred_element_type=jnp.float32).astype(jnp.bfloat16)
        q4 = queries.reshape(SEQ, HEADS, HS).astype(jnp.float32)
        kv4 = kv.reshape(SEQ, KVH, 2, HS).astype(jnp.float32)
        keys = jnp.repeat(kv4[:, :, 0], group, axis=1)
        values = jnp.repeat(kv4[:, :, 1], group, axis=1)
        scores = jnp.einsum('qhd,shd->hqs', q4, keys) * scale
        scores = jnp.where(causal[None], scores, -1e+30)
        top = lax.optimization_barrier(jnp.max(scores, -1, keepdims=True))
        weights = jnp.exp(scores - top)
        probs = weights / lax.optimization_barrier(jnp.sum(weights, -1, keepdims=True))
        probs_low = probs.astype(jnp.bfloat16).astype(jnp.float32)
        attended = jnp.einsum('hqs,shd->qhd', probs_low, values).astype(jnp.bfloat16)
        att_flat = attended.reshape(SEQ, QW)
        partial_value = jnp.einsum('qtc,tcd->tqd', att_flat.astype(jnp.float32).reshape(SEQ, N_TENSOR, cols), out_f)
        partial_value = partial_value.astype(jnp.bfloat16)
        grad_heads = lax.dot_general(cot_a, out_weight, (((1,), (1,)), ((), ())), preferred_element_type=jnp.float32).astype(jnp.bfloat16)
        g4 = grad_heads.reshape(SEQ, HEADS, HS).astype(jnp.float32)
        delta = lax.optimization_barrier(jnp.sum(g4 * attended.astype(jnp.float32), -1)).T
        grad_probs = jnp.einsum('qhd,shd->hqs', g4, values)
        grad_scores = (probs * (grad_probs - delta[:, :, None]) * scale).astype(jnp.bfloat16).astype(jnp.float32)
        grad_q = jnp.einsum('hqs,shd->qhd', grad_scores, keys).astype(jnp.bfloat16)
        grad_keys = jnp.einsum('hqs,qhd->hsd', grad_scores, q4)
        grad_values = jnp.einsum('hqs,qhd->hsd', probs_low, g4)
        part_keys = jnp.einsum('ht,hj,hsd->tjsd', dev_ind, kv_ind, grad_keys).astype(jnp.bfloat16).astype(jnp.float32)
        part_values = jnp.einsum('ht,hj,hsd->tjsd', dev_ind, kv_ind, grad_values).astype(jnp.bfloat16).astype(jnp.float32)
        kv_keys = lax.optimization_barrier(jnp.sum(part_keys, 0))
        kv_values = lax.optimization_barrier(jnp.sum(part_values, 0))
        kv_grad = jnp.stack([kv_keys, kv_values], 1).transpose(2, 0, 1, 3).reshape(SEQ, KVW).astype(jnp.bfloat16)
        grad_flat = grad_q.reshape(SEQ, N_TENSOR, cols).astype(jnp.float32)
        normed_parts = jnp.einsum('qtc,dtc->tqd', grad_flat, query_f).astype(jnp.bfloat16).astype(jnp.float32)
        normed_grad = lax.optimization_barrier(jnp.sum(normed_parts, 0))
        scaled = gain_f * normed_grad
        grad_stream = inv_rms * scaled - stream_f * inv_rms ** 3 * lax.optimization_barrier(jnp.mean(scaled * stream_f, -1, keepdims=True))
        stream_grad = (cot_s.astype(jnp.float32) + grad_stream).astype(jnp.bfloat16)
        term_query = lax.dot_general(normed, grad_q.reshape(SEQ, QW), (((0,), (0,)), ((), ())), preferred_element_type=jnp.float32)
        term_out = lax.dot_general(att_flat, cot_a, (((0,), (0,)), ((), ())), preferred_element_type=jnp.float32)
        acc_query = acc_query + term_query.astype(jnp.bfloat16).astype(jnp.float32)
        acc_out = acc_out + term_out.astype(jnp.bfloat16).astype(jnp.float32)
        return ((acc_query, acc_out), (partial_value, stream_grad, kv_grad))
    items = (stream_in.reshape(N_FSDP, SEQ, D), keys_values.reshape(N_FSDP, SEQ, KVW), cot_stream.reshape(N_FSDP, SEQ, D), cot_attn.reshape(N_FSDP, SEQ, D))
    start = (jnp.zeros((D, QW), jnp.float32), jnp.zeros((QW, D), jnp.float32))
    (acc_query, acc_out), (partials, stream_grads, kv_grads) = lax.scan(one_sequence, start, items)
    attn_partial = partials.transpose(1, 0, 2, 3).reshape(N_TENSOR, TOKENS, D)
    stream_grad = stream_grads.reshape(TOKENS, D)
    kv_grad = kv_grads.reshape(TOKENS, KVW)
    return (stream_out, attn_partial, stream_grad, kv_grad, acc_query.astype(jnp.bfloat16), acc_out.astype(jnp.bfloat16))
```

```python
import math

import jax
import jax.numpy as jnp
from jax import lax
from jax.experimental import pallas as pl
from jax.experimental.pallas import tpu as pltpu
from jax.sharding import Mesh, PartitionSpec as P

HS = 128
GROUP = 4
ZH, Y, ZL, X, CORE = 4, 8, 2, 4, 2
NT = ZL * X * CORE
NF = ZH * Y
TENSOR = ("zl", "x", "c")
FSDP = ("zh", "y")
S = 128
W = 256
D = NT * W
B = D // NF
EXTRA = 16
F32, BF16 = jnp.float32, jnp.bfloat16
VMEM = pl.BlockSpec(memory_space=pltpu.VMEM)


def call(body, outs, flops=0, nbytes=0):
    return pl.pallas_call(
        body,
        out_shape=outs,
        out_specs=jax.tree.map(lambda _: VMEM, outs),
        compiler_params=pltpu.CompilerParams(vmem_limit_bytes=56 * 2**20),
        cost_estimate=pl.CostEstimate(flops=flops, bytes_accessed=nbytes, transcendentals=0),
    )


def arr(*dims, of=BF16):
    return jax.ShapeDtypeStruct(dims, of)


def place(f):
    return (f % Y) * ZH + f // Y


def nn(a, b):
    return lax.dot_general(a, b, (((1,), (0,)), ((), ())), preferred_element_type=F32)


def nt(a, b):
    return lax.dot_general(a, b, (((1,), (1,)), ((), ())), preferred_element_type=F32)


def flip(a):
    return a.astype(F32).T


def pack_weights(wq, wo, out):
    out[:, :W] = wq[...]
    out[:, W:] = flip(wo[...]).astype(BF16)


def pack_forward(stream, cot, partial, out):
    for t in range(NT):
        out[t, :S] = stream[...]
        out[t, S : 2 * S] = cot[...]
        out[t, 2 * S :] = partial[0, :, t * W : (t + 1) * W]


def prepare(got, stream, gain, normed, cot, normed_t, cot_t, inv_out, out_slice):
    squares = jnp.zeros((S, 1), F32)
    pending = jnp.zeros((S, W), F32)
    for t in range(NT):
        block = got[t, :S].astype(F32)
        squares += jnp.sum(block * block, -1, keepdims=True)
        pending += got[t, 2 * S :].astype(F32)
    inv = lax.rsqrt(squares * (1.0 / D) + 1e-05)
    inv_out[...] = jnp.broadcast_to(inv, (S, 128))
    out_slice[...] = (stream[...].astype(F32) + pending).astype(BF16)
    for f in range(NF):
        t, half = f // 2, (f % 2) * B
        at = place(f) * B
        block = got[t, :S, half : half + B].astype(F32)
        block = block * inv * gain[:, f * B : (f + 1) * B].astype(F32)
        normed[:, at : at + B] = block.astype(BF16)
        normed_t[at : at + B] = block.T.astype(BF16)
        piece = got[t, S : 2 * S, half : half + B]
        cot[:, at : at + B] = piece
        cot_t[at : at + B] = flip(piece).astype(BF16)


def attend(normed, cot, normed_t, cot_t, weights, kv, terms, att_out, gq_out, kv_out):
    scale = 1.0 / math.sqrt(HS)
    step = 512

    def gather(i, carry):
        q, g = carry
        k = pl.ds(pl.multiple_of(i * step, step), step)
        q += nn(normed[:, k], weights[k, :W])
        g += nn(cot[:, k], weights[k, W:])
        return q, g

    zero = jnp.zeros((S, W), F32)
    queries, grads = lax.fori_loop(0, D // step, gather, (zero, zero))
    queries, grads = queries.astype(BF16), grads.astype(BF16)
    keys, values = kv[:, :HS], kv[:, HS:]
    causal = lax.broadcasted_iota(jnp.int32, (S, S), 0) >= lax.broadcasted_iota(jnp.int32, (S, S), 1)
    grad_keys = jnp.zeros((S, HS), F32)
    grad_values = jnp.zeros((S, HS), F32)
    for h in range(W // HS):
        at = slice(h * HS, (h + 1) * HS)
        q, g = queries[:, at], grads[:, at]
        scores = jnp.where(causal, nt(q, keys) * scale, -1e30)
        weight = jnp.exp(scores - jnp.max(scores, -1, keepdims=True))
        probs = weight / jnp.sum(weight, -1, keepdims=True)
        low = probs.astype(BF16)
        att = nn(low, values).astype(BF16)
        delta = jnp.sum(g.astype(F32) * att.astype(F32), -1, keepdims=True)
        gs = (probs * (nt(g, values) - delta) * scale).astype(BF16)
        gq_out[:, at] = nn(gs, keys).astype(BF16)
        att_out[:, at] = att
        grad_keys += nn(flip(gs).astype(BF16), q)
        grad_values += nn(flip(low).astype(BF16), g)
    kv_out[:, :HS] = grad_keys.astype(BF16)
    kv_out[:, HS:] = grad_values.astype(BF16)
    att, gq = att_out[...], gq_out[...]

    def scatter(i, _):
        k = pl.ds(pl.multiple_of(i * step, step), step)
        terms[k, :W] = nn(normed_t[k], gq).astype(BF16)
        terms[k, W:] = nn(cot_t[k], att).astype(BF16)
        return 0

    lax.fori_loop(0, D // step, scatter, 0)


def project(att, gq, weights, got, gain, kv_part, out_slice, partial, send):
    rows = jnp.zeros((S, 1), F32)
    for y in range(Y):
        k = slice(y * ZH * B, (y + 1) * ZH * B)
        out = nt(att[...], weights[k, W:]).astype(BF16)
        grad = nt(gq[...], weights[k, :W]).astype(BF16)
        for z in range(ZH):
            f = z * Y + y
            t, half = f // 2, (f % 2) * B
            block = grad[:, z * B : (z + 1) * B]
            partial[0, :, f * B : (f + 1) * B] = out[:, z * B : (z + 1) * B]
            send[t, :S, half : half + B] = block
            stream = got[t, :, half : half + B].astype(F32)
            scaled = gain[:, f * B : (f + 1) * B].astype(F32) * block.astype(F32)
            rows += jnp.sum(scaled * stream, -1, keepdims=True)
    across = jnp.broadcast_to(rows, (S, S)).T[:EXTRA]
    high = across.astype(BF16).astype(F32)
    middle = (across - high).astype(BF16).astype(F32)
    low = across - high - middle
    line = lax.broadcasted_iota(jnp.int32, (EXTRA, S), 0)
    zero = jnp.zeros_like(low)
    pieces = jnp.where(line == 0, high, jnp.where(line == 1, middle, jnp.where(line == 2, low, zero)))
    pieces = jnp.concatenate([pieces, jnp.zeros((EXTRA, W - S), F32)], 1).astype(BF16)
    for t in range(NT):
        send[t, S : 2 * S] = kv_part[...]
        send[t, 2 * S : 3 * S] = out_slice[...]
        send[t, 3 * S :] = pieces


def finish(got, stream, cot_stream, gain, inv_in, stream_out, stream_grad, kv_grad):
    grad = jnp.zeros((S, W), F32)
    lines = jnp.zeros((EXTRA, S), F32)
    for t in range(NT):
        grad += got[t, :S].astype(F32)
        lines += got[t, 3 * S :, :S].astype(F32)
        stream_out[:, t * W : (t + 1) * W] = got[t, 2 * S : 3 * S]
    share = GROUP * HS // W
    for j in range(NT // share):
        total = got[share * j, S : 2 * S].astype(F32)
        for i in range(1, share):
            total += got[share * j + i, S : 2 * S].astype(F32)
        kv_grad[:, j * W : (j + 1) * W] = total.astype(BF16)
    total = jnp.sum(lines, 0, keepdims=True)
    mean = jnp.broadcast_to(total, (S, S)).T[:, :1] * (1.0 / D)
    inv = inv_in[:, :1]
    grad = inv * (gain[...].astype(F32) * grad) - stream[...].astype(F32) * (inv * inv * inv) * mean
    stream_grad[...] = (cot_stream[...].astype(F32) + grad).astype(BF16)


def add_up(got, wq_grad, wo_grad):
    total = got[0].astype(F32)
    for z in range(1, ZH):
        total += got[z].astype(F32)
    wq_grad[...] = total[:, :W].astype(BF16)
    wo_grad[...] = total[:, W:].T.astype(BF16)


def per_device(
    stream_in, newer_partial, norm_gain, query_weight, keys_values, out_weight, cot_stream, cot_attn
):
    rank = lax.axis_index(TENSOR)
    gain = norm_gain.reshape(1, D)
    gain_own = lax.dynamic_slice_in_dim(gain, rank * W, W, 1)
    kv_own = lax.dynamic_slice_in_dim(keys_values, rank * W // HS // GROUP * 2 * HS, 2 * HS, 1)

    weights = call(pack_weights, arr(B, 2 * W))(query_weight, out_weight)
    weights = lax.all_gather(weights, "zh", axis=0, tiled=True)
    weights = lax.all_gather(weights, "y", axis=0, tiled=True)

    send = call(pack_forward, arr(NT, 3 * S, W))(stream_in, cot_attn, newer_partial)
    got = lax.all_to_all(send, TENSOR, 0, 0, tiled=True)
    normed, cot, normed_t, cot_t, inv, out_slice = call(
        prepare, [arr(S, D), arr(S, D), arr(D, S), arr(D, S), arr(S, 128, of=F32), arr(S, W)]
    )(got, stream_in, gain)

    terms, att, gq, kv_part = call(
        attend, [arr(D, 2 * W), arr(S, W), arr(S, W), arr(S, 2 * HS)], flops=8 * S * D * W
    )(normed, cot, normed_t, cot_t, weights, kv_own)

    terms = lax.psum_scatter(terms, "y", scatter_dimension=0, tiled=True)
    terms = lax.all_to_all(terms.reshape(ZH, B, 2 * W), "zh", 0, 0, tiled=True)
    wq_grad, wo_grad = call(add_up, [arr(B, W), arr(W, B)])(terms)

    attn_partial, send = call(
        project, [arr(1, S, D), arr(NT, 3 * S + EXTRA, W)], flops=4 * S * D * W
    )(att, gq, weights, got[:, :S], gain, kv_part, out_slice)
    got = lax.all_to_all(send, TENSOR, 0, 0, tiled=True)
    stream_out, stream_grad, kv_grad = call(finish, [arr(S, D), arr(S, W), arr(*keys_values.shape)])(
        got, stream_in, cot_stream, gain_own, inv
    )
    return (stream_out, attn_partial, stream_grad, kv_grad, wq_grad, wo_grad)


def solution(mesh):
    fine = Mesh(mesh.devices.reshape(ZH, Y, ZL, X, CORE), FSDP + TENSOR)
    return jax.shard_map(
        per_device,
        mesh=fine,
        in_specs=(
            P(FSDP, TENSOR),
            P(TENSOR, FSDP, None),
            P(),
            P(FSDP, TENSOR),
            P(FSDP, None),
            P(TENSOR, FSDP),
            P(FSDP, TENSOR),
            P(FSDP, TENSOR),
        ),
        out_specs=(
            P(FSDP, None),
            P(TENSOR, FSDP, None),
            P(FSDP, TENSOR),
            P(FSDP, None),
            P(FSDP, TENSOR),
            P(TENSOR, FSDP),
        ),
        check_vma=False,
    )
```

```python
import math

import jax
import jax.numpy as jnp
from jax import lax
from jax.experimental import pallas as pl
from jax.experimental.pallas import tpu as pltpu
from jax.sharding import Mesh, PartitionSpec as P

HS = 128
GROUP = 4
ZH, Y, ZL, X, CORE = 4, 8, 2, 4, 2
NT = ZL * X * CORE
NF = ZH * Y
TENSOR = ("zl", "x", "c")
FSDP = ("zh", "y")
S = 128
W = 256
D = NT * W
B = D // NF
EXTRA = 16
F32, BF16 = jnp.float32, jnp.bfloat16
ANY = pl.BlockSpec(memory_space=pl.ANY)
VMEM = pl.BlockSpec(memory_space=pltpu.VMEM)
SMEM = pl.BlockSpec(memory_space=pltpu.SMEM)
R = ZH * B


def call(body, outs, flops=0, nbytes=0, **specs):
    return pl.pallas_call(
        body,
        out_shape=outs,
        compiler_params=pltpu.CompilerParams(vmem_limit_bytes=56 * 2**20),
        cost_estimate=pl.CostEstimate(flops=flops, bytes_accessed=nbytes, transcendentals=0),
        **specs,
    )


def arr(*dims, of=BF16):
    return jax.ShapeDtypeStruct(dims, of)


def place(f):
    return (f % Y) * ZH + f // Y


def nn(a, b):
    return lax.dot_general(a, b, (((1,), (0,)), ((), ())), preferred_element_type=F32)


def nt(a, b):
    return lax.dot_general(a, b, (((1,), (1,)), ((), ())), preferred_element_type=F32)


def flip(a):
    return a.astype(F32).T


def pack_weights(wq, wo, out):
    out[0] = wq[...]
    out[1] = flip(wo[...]).astype(BF16)


def pack_forward(stream, cot, partial, _, out):
    for t in range(NT):
        out[t, :S] = stream[...]
        out[t, S : 2 * S] = cot[...]
        out[t, 2 * S :] = partial[0, :, t * W : (t + 1) * W]


def prepare(got, stream, gain, normed, cot, normed_t, cot_t, inv_out, out_slice):
    squares = jnp.zeros((S, 1), F32)
    pending = jnp.zeros((S, W), F32)
    for t in range(NT):
        block = got[t, :S].astype(F32)
        squares += jnp.sum(block * block, -1, keepdims=True)
        pending += got[t, 2 * S :].astype(F32)
    inv = lax.rsqrt(squares * (1.0 / D) + 1e-05)
    inv_out[...] = jnp.broadcast_to(inv, (S, 128))
    out_slice[...] = (stream[...].astype(F32) + pending).astype(BF16)
    for f in range(NF):
        t, half = f // 2, (f % 2) * B
        at = place(f) * B
        block = got[t, :S, half : half + B].astype(F32)
        block = block * inv * gain[:, f * B : (f + 1) * B].astype(F32)
        normed[:, at : at + B] = block.astype(BF16)
        normed_t[at : at + B] = block.T.astype(BF16)
        piece = got[t, S : 2 * S, half : half + B]
        cot[:, at : at + B] = piece
        cot_t[at : at + B] = flip(piece).astype(BF16)


def rows_of(me, distance):
    return lax.rem(me + (distance + Y), Y)


def block(index):
    return pl.ds(pl.multiple_of(index * R, R), R)


FIRST, REST = (4, 3), (5, 2, 6, 1, 7, 0)


def attend(me, normed, cot, normed_t, cot_t, kv, *refs):
    wq, wo = refs[0], refs[1 : Y + 1]
    q_terms, *o_terms = refs[Y + 1 : Y + 4]
    att_out, gq_out, kv_out = refs[Y + 4 :]
    scale = 1.0 / math.sqrt(HS)
    queries = jnp.zeros((S, W), F32)
    grads = jnp.zeros((S, W), F32)
    for d in range(Y):
        k = block(rows_of(me[0], d))
        queries += nn(normed[:, k], wq[k])
        grads += nn(cot[:, k], wo[d][...])
    queries, grads = queries.astype(BF16), grads.astype(BF16)
    keys, values = kv[:, :HS], kv[:, HS:]
    causal = lax.broadcasted_iota(jnp.int32, (S, S), 0) >= lax.broadcasted_iota(jnp.int32, (S, S), 1)
    grad_keys = jnp.zeros((S, HS), F32)
    grad_values = jnp.zeros((S, HS), F32)
    for h in range(W // HS):
        at = slice(h * HS, (h + 1) * HS)
        q, g = queries[:, at], grads[:, at]
        scores = jnp.where(causal, nt(q, keys) * scale, -1e30)
        weight = jnp.exp(scores - jnp.max(scores, -1, keepdims=True))
        probs = weight / jnp.sum(weight, -1, keepdims=True)
        low = probs.astype(BF16)
        att = nn(low, values).astype(BF16)
        delta = jnp.sum(g.astype(F32) * att.astype(F32), -1, keepdims=True)
        gs = (probs * (nt(g, values) - delta) * scale).astype(BF16)
        gq_out[:, at] = nn(gs, keys).astype(BF16)
        att_out[:, at] = att
        grad_keys += nn(flip(gs).astype(BF16), q)
        grad_values += nn(flip(low).astype(BF16), g)
    kv_out[:, :HS] = grad_keys.astype(BF16)
    kv_out[:, HS:] = grad_values.astype(BF16)
    write_terms(me, cot_t, att_out, o_terms, FIRST)
    gq = gq_out[...]
    for y in range(Y):
        q_terms[y * R : (y + 1) * R] = nn(normed_t[y * R : (y + 1) * R], gq).astype(BF16)


def write_terms(me, cot_t, att, outs, distances):
    for d, out in zip(distances, outs):
        out[...] = nn(cot_t[block(rows_of(me[0], d))], att[...]).astype(BF16)


def attend_rest(me, cot_t, att, *outs):
    write_terms(me, cot_t, att, outs, REST)


def project(me, att, gq, got, gain, kv_part, out_slice, *refs):
    wq, wo, (partial, send) = refs[0], refs[1 : Y + 1], refs[Y + 1 :]
    rows = jnp.zeros((S, 1), F32)
    for d in range(Y):
        y = rows_of(me[0], d)
        out = nt(att[...], wo[d][...]).astype(BF16)
        grad = nt(gq[...], wq[block(y)]).astype(BF16)
        half = pl.ds(pl.multiple_of(lax.rem(y, 2) * B, B), B)
        for z in range(ZH):
            t = z * (Y // 2) + y // 2
            at = pl.ds(pl.multiple_of((z * Y + y) * B, B), B)
            piece = grad[:, z * B : (z + 1) * B]
            partial[0, :, at] = out[:, z * B : (z + 1) * B]
            send[t, :S, half] = piece
            stream = got[t, :, half].astype(F32)
            scaled = gain[:, at].astype(F32) * piece.astype(F32)
            rows += jnp.sum(scaled * stream, -1, keepdims=True)
    across = jnp.broadcast_to(rows, (S, S)).T[:EXTRA]
    high = across.astype(BF16).astype(F32)
    middle = (across - high).astype(BF16).astype(F32)
    low = across - high - middle
    line = lax.broadcasted_iota(jnp.int32, (EXTRA, S), 0)
    zero = jnp.zeros_like(low)
    pieces = jnp.where(line == 0, high, jnp.where(line == 1, middle, jnp.where(line == 2, low, zero)))
    pieces = jnp.concatenate([pieces, jnp.zeros((EXTRA, W - S), F32)], 1).astype(BF16)
    for t in range(NT):
        send[t, S : 2 * S] = kv_part[...]
        send[t, 2 * S : 3 * S] = out_slice[...]
        send[t, 3 * S :] = pieces


def close(q, own, went_up, went_down, _, out):
    o = own[...].astype(F32) + went_up[...].astype(F32) + went_down[...].astype(F32)
    for z in range(ZH):
        out[z, :B] = q[z * B : (z + 1) * B]
        out[z, B:] = o[z * B : (z + 1) * B].astype(BF16)


def finish(got, stream, cot_stream, gain, inv_in, stream_out, stream_grad, kv_grad):
    grad = jnp.zeros((S, W), F32)
    lines = jnp.zeros((EXTRA, S), F32)
    for t in range(NT):
        grad += got[t, :S].astype(F32)
        lines += got[t, 3 * S :, :S].astype(F32)
        stream_out[:, t * W : (t + 1) * W] = got[t, 2 * S : 3 * S]
    share = GROUP * HS // W
    for j in range(NT // share):
        total = got[share * j, S : 2 * S].astype(F32)
        for i in range(1, share):
            total += got[share * j + i, S : 2 * S].astype(F32)
        kv_grad[:, j * W : (j + 1) * W] = total.astype(BF16)
    total = jnp.sum(lines, 0, keepdims=True)
    mean = jnp.broadcast_to(total, (S, S)).T[:, :1] * (1.0 / D)
    inv = inv_in[:, :1]
    grad = inv * (gain[...].astype(F32) * grad) - stream[...].astype(F32) * (inv * inv * inv) * mean
    stream_grad[...] = (cot_stream[...].astype(F32) + grad).astype(BF16)


def add_up(got, wq_grad, wo_grad):
    total = got[0].astype(F32)
    for z in range(1, ZH):
        total += got[z].astype(F32)
    wq_grad[...] = total[:B].astype(BF16)
    wo_grad[...] = total[B:].T.astype(BF16)


def up(a):
    return lax.ppermute(a, "y", [(i, (i + 1) % Y) for i in range(Y)])


def down(a):
    return lax.ppermute(a, "y", [(i, (i - 1) % Y) for i in range(Y)])


def gather_ring(own):
    blocks = {0: own}
    for step in range(1, 5):
        blocks[step] = down(blocks[step - 1])
        if step < 4:
            blocks[-step % Y] = up(blocks[(1 - step) % Y])
    return [blocks[d] for d in range(Y)]


def plus(a, b):
    return (a.astype(F32) + b.astype(F32)).astype(BF16)


def scatter_ring(terms):
    went_up, went_down = terms[3], terms[4]
    for step in range(3):
        went_down = plus(down(went_down), terms[5 + step])
        went_up = up(went_up)
        if step < 2:
            went_up = plus(went_up, terms[2 - step])
    return terms[0], went_up, down(went_down)


def per_device(
    stream_in, newer_partial, norm_gain, query_weight, keys_values, out_weight, cot_stream, cot_attn
):
    rank = lax.axis_index(TENSOR)
    gain = norm_gain.reshape(1, D)
    gain_own = lax.dynamic_slice_in_dim(gain, rank * W, W, 1)
    kv_own = lax.dynamic_slice_in_dim(keys_values, rank * W // HS // GROUP * 2 * HS, 2 * HS, 1)

    me = lax.axis_index("y").reshape(1)

    weights = call(pack_weights, arr(2, B, W))(query_weight, out_weight)
    weights = lax.all_gather(weights, "zh", axis=1, tiled=True)
    wq = lax.all_gather(weights[0], "y", axis=0, tiled=True)
    wo = gather_ring(weights[1])

    send = call(pack_forward, arr(NT, 3 * S, W), in_specs=[VMEM] * 3 + [ANY])(
        stream_in, cot_attn, newer_partial, weights
    )
    got = lax.all_to_all(send, TENSOR, 0, 0, tiled=True)
    normed, cot, normed_t, cot_t, inv, out_slice = call(
        prepare, [arr(S, D), arr(S, D), arr(D, S), arr(D, S), arr(S, 128, of=F32), arr(S, W)]
    )(got, stream_in, gain)

    term = arr(R, W)
    q_terms, o4, o3, att, gq, kv_part = call(
        attend,
        [arr(D, W), term, term, arr(S, W), arr(S, W), arr(S, 2 * HS)],
        flops=7 * S * D * W,
        in_specs=[SMEM] + [VMEM] * (6 + Y),
    )(me, normed, cot, normed_t, cot_t, kv_own, wq, *wo)
    rest = call(attend_rest, [term] * 6, flops=2 * S * D * W, in_specs=[SMEM] + [VMEM] * 2)(
        me, cot_t, att
    )
    o_terms = {4: o4, 3: o3} | dict(zip(REST, rest))

    streams = pl.BlockSpec((NT, S, W), lambda i: (0, 0, 0))
    attn_partial, send = call(
        project,
        [arr(1, S, D), arr(NT, 3 * S + EXTRA, W)],
        flops=4 * S * D * W,
        grid=(1,),
        in_specs=[SMEM] + [VMEM] * 2 + [streams] + [VMEM] * (4 + Y),
        out_specs=[VMEM, VMEM],
    )(me, att, gq, got, gain, kv_part, out_slice, wq, *wo)
    got = lax.all_to_all(send, TENSOR, 0, 0, tiled=True)
    stream_out, stream_grad, kv_grad = call(finish, [arr(S, D), arr(S, W), arr(*keys_values.shape)])(
        got, stream_in, cot_stream, gain_own, inv
    )

    q_sum = lax.psum_scatter(q_terms, "y", scatter_dimension=0, tiled=True)
    o_sums = scatter_ring(o_terms)
    sums = call(close, arr(ZH, 2 * B, W), in_specs=[VMEM] * 4 + [ANY])(q_sum, *o_sums, got)
    sums = lax.all_to_all(sums, "zh", 0, 0, tiled=True)
    wq_grad, wo_grad = call(add_up, [arr(B, W), arr(W, B)])(sums)
    return (stream_out, attn_partial, stream_grad, kv_grad, wq_grad, wo_grad)


def solution(mesh):
    fine = Mesh(mesh.devices.reshape(ZH, Y, ZL, X, CORE), FSDP + TENSOR)
    return jax.shard_map(
        per_device,
        mesh=fine,
        in_specs=(
            P(FSDP, TENSOR),
            P(TENSOR, FSDP, None),
            P(),
            P(FSDP, TENSOR),
            P(FSDP, None),
            P(TENSOR, FSDP),
            P(FSDP, TENSOR),
            P(FSDP, TENSOR),
        ),
        out_specs=(
            P(FSDP, None),
            P(TENSOR, FSDP, None),
            P(FSDP, TENSOR),
            P(FSDP, None),
            P(FSDP, TENSOR),
            P(TENSOR, FSDP),
        ),
        check_vma=False,
    )
```

```python
import math

import jax
import jax.numpy as jnp
from jax import lax
from jax.experimental import pallas as pl
from jax.experimental.pallas import tpu as pltpu
from jax.sharding import Mesh, PartitionSpec as P

HS = 128
GROUP = 4
ZH, Y, ZL, X, CORE = 4, 8, 2, 4, 2
NT = ZL * X * CORE
NF = ZH * Y
TENSOR = ("zl", "x", "c")
FSDP = ("zh", "y")
S = 128
W = 256
D = NT * W
B = D // NF
EXTRA = 16
F32, BF16 = jnp.float32, jnp.bfloat16
HBM = pl.BlockSpec(memory_space=pltpu.HBM)
VMEM = pl.BlockSpec(memory_space=pltpu.VMEM)
STEP = 512


def call(body, outs, mib, flops=0, nbytes=0, **specs):
    return pl.pallas_call(
        body,
        out_shape=outs,
        compiler_params=pltpu.CompilerParams(vmem_limit_bytes=mib * 2**20),
        cost_estimate=pl.CostEstimate(flops=flops, bytes_accessed=nbytes, transcendentals=0),
        **specs,
    )


def arr(*dims, of=BF16):
    return jax.ShapeDtypeStruct(dims, of)


def place(f):
    return (f % Y) * ZH + f // Y


def nn(a, b):
    return lax.dot_general(a, b, (((1,), (0,)), ((), ())), preferred_element_type=F32)


def nt(a, b):
    return lax.dot_general(a, b, (((1,), (1,)), ((), ())), preferred_element_type=F32)


def flip(a):
    return a.astype(F32).T


def pack_weights(wq, wo, out):
    out[:, :W] = wq[...]
    out[:, W:] = flip(wo[...]).astype(BF16)


def pack_forward(stream, cot, partial, out):
    for t in range(NT):
        out[t, :S] = stream[...]
        out[t, S : 2 * S] = cot[...]
        out[t, 2 * S :] = partial[0, :, t * W : (t + 1) * W]


def prepare(got, stream, gain, normed, cot, normed_t, cot_t, inv_out, out_slice):
    squares = jnp.zeros((S, 1), F32)
    pending = jnp.zeros((S, W), F32)
    for t in range(NT):
        block = got[t, :S].astype(F32)
        squares += jnp.sum(block * block, -1, keepdims=True)
        pending += got[t, 2 * S :].astype(F32)
    inv = lax.rsqrt(squares * (1.0 / D) + 1e-05)
    inv_out[...] = jnp.broadcast_to(inv, (S, 128))
    out_slice[...] = (stream[...].astype(F32) + pending).astype(BF16)
    for f in range(NF):
        t, half = f // 2, (f % 2) * B
        at = place(f) * B
        block = got[t, :S, half : half + B].astype(F32)
        block = block * inv * gain[:, f * B : (f + 1) * B].astype(F32)
        normed[:, at : at + B] = block.astype(BF16)
        normed_t[at : at + B] = block.T.astype(BF16)
        piece = got[t, S : 2 * S, half : half + B]
        cot[:, at : at + B] = piece
        cot_t[at : at + B] = flip(piece).astype(BF16)


def attend(
    normed, cot, normed_t, cot_t, weights, kv, terms, att_out, gq_out, kv_out, w_held, t_held, w_sem, t_sem
):
    scale = 1.0 / math.sqrt(HS)
    chunks = [slice(i * STEP, (i + 1) * STEP) for i in range(D // STEP)]
    arrived = [
        pltpu.make_async_copy(weights.at[k], w_held.at[k], w_sem.at[i]) for i, k in enumerate(chunks)
    ]
    for copy in arrived:
        copy.start()
    queries = jnp.zeros((S, W), F32)
    grads = jnp.zeros((S, W), F32)
    for copy, k in zip(arrived, chunks):
        copy.wait()
        queries += nn(normed[:, k], w_held[k, :W])
        grads += nn(cot[:, k], w_held[k, W:])
    queries, grads = queries.astype(BF16), grads.astype(BF16)
    keys, values = kv[:, :HS], kv[:, HS:]
    causal = lax.broadcasted_iota(jnp.int32, (S, S), 0) >= lax.broadcasted_iota(jnp.int32, (S, S), 1)
    grad_keys = jnp.zeros((S, HS), F32)
    grad_values = jnp.zeros((S, HS), F32)
    for h in range(W // HS):
        at = slice(h * HS, (h + 1) * HS)
        q, g = queries[:, at], grads[:, at]
        scores = jnp.where(causal, nt(q, keys) * scale, -1e30)
        weight = jnp.exp(scores - jnp.max(scores, -1, keepdims=True))
        probs = weight / jnp.sum(weight, -1, keepdims=True)
        low = probs.astype(BF16)
        att = nn(low, values).astype(BF16)
        delta = jnp.sum(g.astype(F32) * att.astype(F32), -1, keepdims=True)
        gs = (probs * (nt(g, values) - delta) * scale).astype(BF16)
        gq_out[:, at] = nn(gs, keys).astype(BF16)
        att_out[:, at] = att
        grad_keys += nn(flip(gs).astype(BF16), q)
        grad_values += nn(flip(low).astype(BF16), g)
    kv_out[:, :HS] = grad_keys.astype(BF16)
    kv_out[:, HS:] = grad_values.astype(BF16)
    att, gq = att_out[...], gq_out[...]
    leaving = []
    for i, k in enumerate(chunks):
        t_held[k, :W] = nn(normed_t[k], gq).astype(BF16)
        t_held[k, W:] = nn(cot_t[k], att).astype(BF16)
        leaving.append(pltpu.make_async_copy(t_held.at[k], terms.at[k], t_sem.at[i]))
        leaving[-1].start()
    for copy in leaving:
        copy.wait()


def project(att, gq, weights, got, gain, kv_part, out_slice, partial, send):
    rows = jnp.zeros((S, 1), F32)
    for y in range(Y):
        k = slice(y * ZH * B, (y + 1) * ZH * B)
        out = nt(att[...], weights[k, W:]).astype(BF16)
        grad = nt(gq[...], weights[k, :W]).astype(BF16)
        for z in range(ZH):
            f = z * Y + y
            t, half = f // 2, (f % 2) * B
            block = grad[:, z * B : (z + 1) * B]
            partial[0, :, f * B : (f + 1) * B] = out[:, z * B : (z + 1) * B]
            send[t, :S, half : half + B] = block
            stream = got[t, :, half : half + B].astype(F32)
            scaled = gain[:, f * B : (f + 1) * B].astype(F32) * block.astype(F32)
            rows += jnp.sum(scaled * stream, -1, keepdims=True)
    across = jnp.broadcast_to(rows, (S, S)).T[:EXTRA]
    high = across.astype(BF16).astype(F32)
    middle = (across - high).astype(BF16).astype(F32)
    low = across - high - middle
    line = lax.broadcasted_iota(jnp.int32, (EXTRA, S), 0)
    zero = jnp.zeros_like(low)
    pieces = jnp.where(line == 0, high, jnp.where(line == 1, middle, jnp.where(line == 2, low, zero)))
    pieces = jnp.concatenate([pieces, jnp.zeros((EXTRA, W - S), F32)], 1).astype(BF16)
    for t in range(NT):
        send[t, S : 2 * S] = kv_part[...]
        send[t, 2 * S : 3 * S] = out_slice[...]
        send[t, 3 * S :] = pieces


def finish(got, stream, cot_stream, gain, inv_in, stream_out, stream_grad, kv_grad):
    grad = jnp.zeros((S, W), F32)
    lines = jnp.zeros((EXTRA, S), F32)
    for t in range(NT):
        grad += got[t, :S].astype(F32)
        lines += got[t, 3 * S :, :S].astype(F32)
        stream_out[:, t * W : (t + 1) * W] = got[t, 2 * S : 3 * S]
    share = GROUP * HS // W
    for j in range(NT // share):
        total = got[share * j, S : 2 * S].astype(F32)
        for i in range(1, share):
            total += got[share * j + i, S : 2 * S].astype(F32)
        kv_grad[:, j * W : (j + 1) * W] = total.astype(BF16)
    total = jnp.sum(lines, 0, keepdims=True)
    mean = jnp.broadcast_to(total, (S, S)).T[:, :1] * (1.0 / D)
    inv = inv_in[:, :1]
    grad = inv * (gain[...].astype(F32) * grad) - stream[...].astype(F32) * (inv * inv * inv) * mean
    stream_grad[...] = (cot_stream[...].astype(F32) + grad).astype(BF16)


def add_up(got, wq_grad, wo_grad):
    total = got[0].astype(F32)
    for z in range(1, ZH):
        total += got[z].astype(F32)
    wq_grad[...] = total[:, :W].astype(BF16)
    wo_grad[...] = total[:, W:].T.astype(BF16)


def per_device(
    stream_in, newer_partial, norm_gain, query_weight, keys_values, out_weight, cot_stream, cot_attn
):
    rank = lax.axis_index(TENSOR)
    gain = norm_gain.reshape(1, D)
    gain_own = lax.dynamic_slice_in_dim(gain, rank * W, W, 1)
    kv_own = lax.dynamic_slice_in_dim(keys_values, rank * W // HS // GROUP * 2 * HS, 2 * HS, 1)

    weights = call(pack_weights, arr(B, 2 * W), 4)(query_weight, out_weight)
    weights = lax.all_gather(weights, "zh", axis=0, tiled=True)
    weights = lax.all_gather(weights, "y", axis=0, tiled=True)

    send = call(pack_forward, arr(NT, 3 * S, W), 10)(stream_in, cot_attn, newer_partial)
    got = lax.all_to_all(send, TENSOR, 0, 0, tiled=True)
    normed, cot, normed_t, cot_t, inv, out_slice = call(
        prepare, [arr(S, D), arr(S, D), arr(D, S), arr(D, S), arr(S, 128, of=F32), arr(S, W)], 14
    )(got, stream_in, gain)

    terms, att, gq, kv_part = call(
        attend,
        [arr(D, 2 * W), arr(S, W), arr(S, W), arr(S, 2 * HS)],
        48,
        flops=8 * S * D * W,
        in_specs=[VMEM] * 4 + [HBM, VMEM],
        out_specs=[HBM] + [VMEM] * 3,
        scratch_shapes=[
            pltpu.VMEM((D, 2 * W), BF16),
            pltpu.VMEM((D, 2 * W), BF16),
            pltpu.SemaphoreType.DMA((D // STEP,)),
            pltpu.SemaphoreType.DMA((D // STEP,)),
        ],
    )(normed, cot, normed_t, cot_t, weights, kv_own)

    terms = lax.psum_scatter(terms, "y", scatter_dimension=0, tiled=True)
    terms = lax.all_to_all(terms.reshape(ZH, B, 2 * W), "zh", 0, 0, tiled=True)
    wq_grad, wo_grad = call(add_up, [arr(B, W), arr(W, B)], 4)(terms)

    streams = pl.BlockSpec((NT, S, W), lambda i: (0, 0, 0))
    attn_partial, send = call(
        project,
        [arr(1, S, D), arr(NT, 3 * S + EXTRA, W)],
        22,
        flops=4 * S * D * W,
        grid=(1,),
        in_specs=[VMEM] * 3 + [streams] + [VMEM] * 3,
        out_specs=[VMEM, VMEM],
    )(att, gq, weights, got, gain, kv_part, out_slice)
    got = lax.all_to_all(send, TENSOR, 0, 0, tiled=True)
    stream_out, stream_grad, kv_grad = call(
        finish, [arr(S, D), arr(S, W), arr(*keys_values.shape)], 12
    )(got, stream_in, cot_stream, gain_own, inv)
    return (stream_out, attn_partial, stream_grad, kv_grad, wq_grad, wo_grad)


def solution(mesh):
    fine = Mesh(mesh.devices.reshape(ZH, Y, ZL, X, CORE), FSDP + TENSOR)
    return jax.shard_map(
        per_device,
        mesh=fine,
        in_specs=(
            P(FSDP, TENSOR),
            P(TENSOR, FSDP, None),
            P(),
            P(FSDP, TENSOR),
            P(FSDP, None),
            P(TENSOR, FSDP),
            P(FSDP, TENSOR),
            P(FSDP, TENSOR),
        ),
        out_specs=(
            P(FSDP, None),
            P(TENSOR, FSDP, None),
            P(FSDP, TENSOR),
            P(FSDP, None),
            P(FSDP, TENSOR),
            P(TENSOR, FSDP),
        ),
        check_vma=False,
    )
```

```python
import math

import jax
import jax.numpy as jnp
from jax import lax
from jax.experimental import pallas as pl
from jax.experimental.pallas import tpu as pltpu
from jax.sharding import Mesh, PartitionSpec as P

HS = 128
GROUP = 4
ZH, Y, ZL, X, CORE = 4, 8, 2, 4, 2
NT = ZL * X * CORE
NF = ZH * Y
TENSOR = ("zl", "x", "c")
FSDP = ("zh", "y")
S = 128
W = 256
D = NT * W
B = D // NF
EXTRA = 16
F32, BF16 = jnp.float32, jnp.bfloat16
HBM = pl.BlockSpec(memory_space=pltpu.HBM)
VMEM = pl.BlockSpec(memory_space=pltpu.VMEM)
STEP = 512


def call(body, outs, mib, flops=0, nbytes=0, **specs):
    return pl.pallas_call(
        body,
        out_shape=outs,
        compiler_params=pltpu.CompilerParams(vmem_limit_bytes=mib * 2**20),
        cost_estimate=pl.CostEstimate(flops=flops, bytes_accessed=nbytes, transcendentals=0),
        **specs,
    )


def arr(*dims, of=BF16):
    return jax.ShapeDtypeStruct(dims, of)


def place(f):
    return (f % Y) * ZH + f // Y


def nn(a, b):
    return lax.dot_general(a, b, (((1,), (0,)), ((), ())), preferred_element_type=F32)


def nt(a, b):
    return lax.dot_general(a, b, (((1,), (1,)), ((), ())), preferred_element_type=F32)


def flip(a):
    return a.astype(F32).T


def pack_weights(wq, wo, out, wo_held, sem):
    copies = [pltpu.make_async_copy(wo, wo_held, sem.at[0]), pltpu.make_async_copy(wq, out.at[:, :W], sem.at[1])]
    for copy in copies:
        copy.start()
    copies[0].wait()
    out[:, W:] = flip(wo_held[...]).astype(BF16)
    copies[1].wait()


def pack_forward(stream, cot, partial, out):
    for t in range(NT):
        out[t, :S] = stream[...]
        out[t, S : 2 * S] = cot[...]
        out[t, 2 * S :] = partial[0, :, t * W : (t + 1) * W]


def prepare(got, stream, gain, normed, cot, normed_t, cot_t, inv_out, out_slice):
    squares = jnp.zeros((S, 1), F32)
    pending = jnp.zeros((S, W), F32)
    for t in range(NT):
        block = got[t, :S].astype(F32)
        squares += jnp.sum(block * block, -1, keepdims=True)
        pending += got[t, 2 * S :].astype(F32)
    inv = lax.rsqrt(squares * (1.0 / D) + 1e-05)
    inv_out[...] = jnp.broadcast_to(inv, (S, 128))
    out_slice[...] = (stream[...].astype(F32) + pending).astype(BF16)
    for f in range(NF):
        t, half = f // 2, (f % 2) * B
        at = place(f) * B
        block = got[t, :S, half : half + B].astype(F32)
        block = block * inv * gain[:, f * B : (f + 1) * B].astype(F32)
        normed[:, at : at + B] = block.astype(BF16)
        normed_t[at : at + B] = block.T.astype(BF16)
        piece = got[t, S : 2 * S, half : half + B]
        cot[:, at : at + B] = piece
        cot_t[at : at + B] = flip(piece).astype(BF16)


def attend(
    normed_in, cot_in, normed_t_in, cot_t_in, weights, kv,
    terms, kept,
    normed, cot, normed_t, cot_t, w_held, t_held, sem, w_sem, t_sem,
):
    scale = 1.0 / math.sqrt(HS)
    chunks = [slice(i * STEP, (i + 1) * STEP) for i in range(D // STEP)]
    pairs = ((normed_in, normed), (cot_in, cot), (normed_t_in, normed_t), (cot_t_in, cot_t))
    brought = [pltpu.make_async_copy(a, b, sem.at[i]) for i, (a, b) in enumerate(pairs)]
    arrived = [
        pltpu.make_async_copy(weights.at[k], w_held.at[k], w_sem.at[i]) for i, k in enumerate(chunks)
    ]
    for copy in brought[:2] + arrived + brought[2:]:
        copy.start()
    queries = jnp.zeros((S, W), F32)
    grads = jnp.zeros((S, W), F32)
    for copy in brought[:2]:
        copy.wait()
    for copy, k in zip(arrived, chunks):
        copy.wait()
        queries += nn(normed[:, k], w_held[k, :W])
        grads += nn(cot[:, k], w_held[k, W:])
    queries, grads = queries.astype(BF16), grads.astype(BF16)
    att_out, gq_out, low_out, gs_out = (kept.at[i] for i in range(4))
    kept[4] = queries
    kept[5] = grads
    keys, values = kv[:, :HS], kv[:, HS:]
    causal = lax.broadcasted_iota(jnp.int32, (S, S), 0) >= lax.broadcasted_iota(jnp.int32, (S, S), 1)
    for h in range(W // HS):
        at = slice(h * HS, (h + 1) * HS)
        q, g = queries[:, at], grads[:, at]
        scores = jnp.where(causal, nt(q, keys) * scale, -1e30)
        weight = jnp.exp(scores - jnp.max(scores, -1, keepdims=True))
        probs = weight / jnp.sum(weight, -1, keepdims=True)
        low = probs.astype(BF16)
        att = nn(low, values).astype(BF16)
        delta = jnp.sum(g.astype(F32) * att.astype(F32), -1, keepdims=True)
        gs = (probs * (nt(g, values) - delta) * scale).astype(BF16)
        gq_out[:, at] = nn(gs, keys).astype(BF16)
        att_out[:, at] = att
        low_out[:, at] = low
        gs_out[:, at] = gs
    att, gq = att_out[...], gq_out[...]
    for copy in brought[2:]:
        copy.wait()
    leaving = []
    for i, k in enumerate(chunks):
        t_held[k, :W] = nn(normed_t[k], gq).astype(BF16)
        t_held[k, W:] = nn(cot_t[k], att).astype(BF16)
        leaving.append(pltpu.make_async_copy(t_held.at[k], terms.at[k], t_sem.at[i]))
        leaving[-1].start()
    for copy in leaving:
        copy.wait()


def project(kept, weights, got, gain, out_slice, partial, send):
    att, gq, low, gs, q, g = (kept.at[i] for i in range(6))
    grad_keys = jnp.zeros((S, HS), F32)
    grad_values = jnp.zeros((S, HS), F32)
    for h in range(W // HS):
        at = slice(h * HS, (h + 1) * HS)
        grad_keys += nn(flip(gs[:, at]).astype(BF16), q[:, at])
        grad_values += nn(flip(low[:, at]).astype(BF16), g[:, at])
    kv_part = jnp.concatenate([grad_keys, grad_values], 1).astype(BF16)
    rows = jnp.zeros((S, 1), F32)
    for y in range(Y):
        k = slice(y * ZH * B, (y + 1) * ZH * B)
        out = nt(att[...], weights[k, W:]).astype(BF16)
        grad = nt(gq[...], weights[k, :W]).astype(BF16)
        for z in range(ZH):
            f = z * Y + y
            t, half = f // 2, (f % 2) * B
            block = grad[:, z * B : (z + 1) * B]
            partial[0, :, f * B : (f + 1) * B] = out[:, z * B : (z + 1) * B]
            send[t, :S, half : half + B] = block
            stream = got[t, :, half : half + B].astype(F32)
            scaled = gain[:, f * B : (f + 1) * B].astype(F32) * block.astype(F32)
            rows += jnp.sum(scaled * stream, -1, keepdims=True)
    across = jnp.broadcast_to(rows, (S, S)).T[:EXTRA]
    high = across.astype(BF16).astype(F32)
    middle = (across - high).astype(BF16).astype(F32)
    rest = across - high - middle
    line = lax.broadcasted_iota(jnp.int32, (EXTRA, S), 0)
    zero = jnp.zeros_like(rest)
    pieces = jnp.where(line == 0, high, jnp.where(line == 1, middle, jnp.where(line == 2, rest, zero)))
    pieces = jnp.concatenate([pieces, jnp.zeros((EXTRA, W - S), F32)], 1).astype(BF16)
    for t in range(NT):
        send[t, S : 2 * S] = kv_part
        send[t, 2 * S : 3 * S] = out_slice[...]
        send[t, 3 * S :] = pieces


def finish(got, stream, cot_stream, gain, inv_in, stream_out, stream_grad, kv_grad):
    grad = jnp.zeros((S, W), F32)
    lines = jnp.zeros((EXTRA, S), F32)
    for t in range(NT):
        grad += got[t, :S].astype(F32)
        lines += got[t, 3 * S :, :S].astype(F32)
        stream_out[:, t * W : (t + 1) * W] = got[t, 2 * S : 3 * S]
    share = GROUP * HS // W
    for j in range(NT // share):
        total = got[share * j, S : 2 * S].astype(F32)
        for i in range(1, share):
            total += got[share * j + i, S : 2 * S].astype(F32)
        kv_grad[:, j * W : (j + 1) * W] = total.astype(BF16)
    total = jnp.sum(lines, 0, keepdims=True)
    mean = jnp.broadcast_to(total, (S, S)).T[:, :1] * (1.0 / D)
    inv = inv_in[:, :1]
    grad = inv * (gain[...].astype(F32) * grad) - stream[...].astype(F32) * (inv * inv * inv) * mean
    stream_grad[...] = (cot_stream[...].astype(F32) + grad).astype(BF16)


def add_up(got, wq_grad, wo_grad):
    total = got[0].astype(F32)
    for z in range(1, ZH):
        total += got[z].astype(F32)
    wq_grad[...] = total[:, :W].astype(BF16)
    wo_grad[...] = total[:, W:].T.astype(BF16)


def per_device(
    stream_in, newer_partial, norm_gain, query_weight, keys_values, out_weight, cot_stream, cot_attn
):
    rank = lax.axis_index(TENSOR)
    gain = norm_gain.reshape(1, D)
    gain_own = lax.dynamic_slice_in_dim(gain, rank * W, W, 1)
    kv_own = lax.dynamic_slice_in_dim(keys_values, rank * W // HS // GROUP * 2 * HS, 2 * HS, 1)

    weights = call(
        pack_weights,
        arr(B, 2 * W),
        56,
        in_specs=[HBM] * 2,
        out_specs=VMEM,
        scratch_shapes=[pltpu.VMEM((W, B), BF16), pltpu.SemaphoreType.DMA((2,))],
    )(query_weight, out_weight)
    weights = lax.all_gather(weights, "zh", axis=0, tiled=True)
    weights = lax.all_gather(weights, "y", axis=0, tiled=True)

    send = call(pack_forward, arr(NT, 3 * S, W), 10)(stream_in, cot_attn, newer_partial)
    got = lax.all_to_all(send, TENSOR, 0, 0, tiled=True)
    normed, cot, normed_t, cot_t, inv, out_slice = call(
        prepare, [arr(S, D), arr(S, D), arr(D, S), arr(D, S), arr(S, 128, of=F32), arr(S, W)], 56
    )(got, stream_in, gain)

    terms, kept = call(
        attend,
        [arr(D, 2 * W), arr(6, S, W)],
        56,
        flops=8 * S * D * W,
        in_specs=[HBM] * 5 + [VMEM],
        out_specs=[HBM, VMEM],
        scratch_shapes=[
            pltpu.VMEM((S, D), BF16),
            pltpu.VMEM((S, D), BF16),
            pltpu.VMEM((D, S), BF16),
            pltpu.VMEM((D, S), BF16),
            pltpu.VMEM((D, 2 * W), BF16),
            pltpu.VMEM((D, 2 * W), BF16),
            pltpu.SemaphoreType.DMA((4,)),
            pltpu.SemaphoreType.DMA((D // STEP,)),
            pltpu.SemaphoreType.DMA((D // STEP,)),
        ],
    )(normed, cot, normed_t, cot_t, weights, kv_own)

    terms = lax.psum_scatter(terms, "y", scatter_dimension=0, tiled=True)
    terms = lax.all_to_all(terms.reshape(ZH, B, 2 * W), "zh", 0, 0, tiled=True)
    wq_grad, wo_grad = call(add_up, [arr(B, W), arr(W, B)], 4)(terms)

    streams = pl.BlockSpec((NT, S, W), lambda i: (0, 0, 0))
    attn_partial, send = call(
        project,
        [arr(1, S, D), arr(NT, 3 * S + EXTRA, W)],
        56,
        flops=4 * S * D * W,
        grid=(1,),
        in_specs=[VMEM] * 2 + [streams] + [VMEM] * 2,
        out_specs=[VMEM, VMEM],
    )(kept, weights, got, gain, out_slice)
    got = lax.all_to_all(send, TENSOR, 0, 0, tiled=True)
    stream_out, stream_grad, kv_grad = call(
        finish, [arr(S, D), arr(S, W), arr(*keys_values.shape)], 12
    )(got, stream_in, cot_stream, gain_own, inv)
    return (stream_out, attn_partial, stream_grad, kv_grad, wq_grad, wo_grad)


def solution(mesh):
    fine = Mesh(mesh.devices.reshape(ZH, Y, ZL, X, CORE), FSDP + TENSOR)
    return jax.shard_map(
        per_device,
        mesh=fine,
        in_specs=(
            P(FSDP, TENSOR),
            P(TENSOR, FSDP, None),
            P(),
            P(FSDP, TENSOR),
            P(FSDP, None),
            P(TENSOR, FSDP),
            P(FSDP, TENSOR),
            P(FSDP, TENSOR),
        ),
        out_specs=(
            P(FSDP, None),
            P(TENSOR, FSDP, None),
            P(FSDP, TENSOR),
            P(FSDP, None),
            P(FSDP, TENSOR),
            P(TENSOR, FSDP),
        ),
        check_vma=False,
    )
```

```python
import math

import jax
import jax.numpy as jnp
from jax import lax
from jax.experimental import pallas as pl
from jax.experimental.pallas import tpu as pltpu
from jax.sharding import Mesh, PartitionSpec as P

HS = 128
GROUP = 4
ZH, Y, ZL, X, CORE = 4, 8, 2, 4, 2
NT = ZL * X * CORE
NF = ZH * Y
TENSOR = ("zl", "x", "c")
FSDP = ("zh", "y")
S = 128
W = 256
D = NT * W
B = D // NF
EXTRA = 16
F32, BF16 = jnp.float32, jnp.bfloat16
ANY = pl.BlockSpec(memory_space=pl.ANY)
HBM = pl.BlockSpec(memory_space=pltpu.HBM)
VMEM = pl.BlockSpec(memory_space=pltpu.VMEM)
STEP = 512


def call(body, outs, mib, flops=0, nbytes=0, **specs):
    return pl.pallas_call(
        body,
        out_shape=outs,
        compiler_params=pltpu.CompilerParams(vmem_limit_bytes=mib * 2**20),
        cost_estimate=pl.CostEstimate(flops=flops, bytes_accessed=nbytes, transcendentals=0),
        **specs,
    )


def arr(*dims, of=BF16):
    return jax.ShapeDtypeStruct(dims, of)


def place(f):
    return (f % Y) * ZH + f // Y


def nn(a, b):
    return lax.dot_general(a, b, (((1,), (0,)), ((), ())), preferred_element_type=F32)


def nt(a, b):
    return lax.dot_general(a, b, (((1,), (1,)), ((), ())), preferred_element_type=F32)


def flip(a):
    return a.astype(F32).T


def pack_weights(wq, wo, out, wo_held, sem):
    copies = [pltpu.make_async_copy(wo, wo_held, sem.at[0]), pltpu.make_async_copy(wq, out.at[:, :W], sem.at[1])]
    for copy in copies:
        copy.start()
    copies[0].wait()
    out[:, W:] = flip(wo_held[...]).astype(BF16)
    copies[1].wait()


def pack_forward(stream, cot, out):
    for t in range(NT):
        out[t, :S] = stream[...]
        out[t, S:] = cot[...]


def pack_partial(partial, _, out):
    for t in range(NT):
        out[t] = partial[0, :, t * W : (t + 1) * W]


def prepare(got, gain, normed, cot, normed_t, cot_t, inv_out):
    squares = jnp.zeros((S, 1), F32)
    for t in range(NT):
        block = got[t, :S].astype(F32)
        squares += jnp.sum(block * block, -1, keepdims=True)
    inv = lax.rsqrt(squares * (1.0 / D) + 1e-05)
    inv_out[...] = jnp.broadcast_to(inv, (S, 128))
    for f in range(NF):
        t, half = f // 2, (f % 2) * B
        at = place(f) * B
        block = got[t, :S, half : half + B].astype(F32)
        block = block * inv * gain[:, f * B : (f + 1) * B].astype(F32)
        normed[:, at : at + B] = block.astype(BF16)
        normed_t[at : at + B] = block.T.astype(BF16)
        piece = got[t, S : 2 * S, half : half + B]
        cot[:, at : at + B] = piece
        cot_t[at : at + B] = flip(piece).astype(BF16)


def attend(normed, cot, normed_t, cot_t, weights, kv, terms, kept, w_held, t_held, w_sem, t_sem):
    scale = 1.0 / math.sqrt(HS)
    chunks = [slice(i * STEP, (i + 1) * STEP) for i in range(D // STEP)]
    arrived = [
        pltpu.make_async_copy(weights.at[k], w_held.at[k], w_sem.at[i]) for i, k in enumerate(chunks)
    ]
    for copy in arrived:
        copy.start()
    queries = jnp.zeros((S, W), F32)
    grads = jnp.zeros((S, W), F32)
    for copy, k in zip(arrived, chunks):
        copy.wait()
        queries += nn(normed[:, k], w_held[k, :W])
        grads += nn(cot[:, k], w_held[k, W:])
    queries, grads = queries.astype(BF16), grads.astype(BF16)
    att_out, gq_out, low_out, gs_out = (kept.at[i] for i in range(4))
    kept[4] = queries
    kept[5] = grads
    keys, values = kv[:, :HS], kv[:, HS:]
    causal = lax.broadcasted_iota(jnp.int32, (S, S), 0) >= lax.broadcasted_iota(jnp.int32, (S, S), 1)
    for h in range(W // HS):
        at = slice(h * HS, (h + 1) * HS)
        q, g = queries[:, at], grads[:, at]
        scores = jnp.where(causal, nt(q, keys) * scale, -1e30)
        weight = jnp.exp(scores - jnp.max(scores, -1, keepdims=True))
        probs = weight / jnp.sum(weight, -1, keepdims=True)
        low = probs.astype(BF16)
        att = nn(low, values).astype(BF16)
        delta = jnp.sum(g.astype(F32) * att.astype(F32), -1, keepdims=True)
        gs = (probs * (nt(g, values) - delta) * scale).astype(BF16)
        gq_out[:, at] = nn(gs, keys).astype(BF16)
        att_out[:, at] = att
        low_out[:, at] = low
        gs_out[:, at] = gs
    att, gq = att_out[...], gq_out[...]
    leaving = []
    for i, k in enumerate(chunks):
        t_held[k, :W] = nn(normed_t[k], gq).astype(BF16)
        t_held[k, W:] = nn(cot_t[k], att).astype(BF16)
        leaving.append(pltpu.make_async_copy(t_held.at[k], terms.at[k], t_sem.at[i]))
        leaving[-1].start()
    for copy in leaving:
        copy.wait()


def project(kept, weights, got, gain, own, pieces_in, partial, send):
    pending = jnp.zeros((S, W), F32)
    for t in range(NT):
        pending += pieces_in[t].astype(F32)
    out_slice = (own[...].astype(F32) + pending).astype(BF16)
    att, gq, low, gs, q, g = (kept.at[i] for i in range(6))
    grad_keys = jnp.zeros((S, HS), F32)
    grad_values = jnp.zeros((S, HS), F32)
    for h in range(W // HS):
        at = slice(h * HS, (h + 1) * HS)
        grad_keys += nn(flip(gs[:, at]).astype(BF16), q[:, at])
        grad_values += nn(flip(low[:, at]).astype(BF16), g[:, at])
    kv_part = jnp.concatenate([grad_keys, grad_values], 1).astype(BF16)
    rows = jnp.zeros((S, 1), F32)
    for y in range(Y):
        k = slice(y * ZH * B, (y + 1) * ZH * B)
        out = nt(att[...], weights[k, W:]).astype(BF16)
        grad = nt(gq[...], weights[k, :W]).astype(BF16)
        for z in range(ZH):
            f = z * Y + y
            t, half = f // 2, (f % 2) * B
            block = grad[:, z * B : (z + 1) * B]
            partial[0, :, f * B : (f + 1) * B] = out[:, z * B : (z + 1) * B]
            send[t, :S, half : half + B] = block
            stream = got[t, :, half : half + B].astype(F32)
            scaled = gain[:, f * B : (f + 1) * B].astype(F32) * block.astype(F32)
            rows += jnp.sum(scaled * stream, -1, keepdims=True)
    across = jnp.broadcast_to(rows, (S, S)).T[:EXTRA]
    high = across.astype(BF16).astype(F32)
    middle = (across - high).astype(BF16).astype(F32)
    rest = across - high - middle
    line = lax.broadcasted_iota(jnp.int32, (EXTRA, S), 0)
    zero = jnp.zeros_like(rest)
    pieces = jnp.where(line == 0, high, jnp.where(line == 1, middle, jnp.where(line == 2, rest, zero)))
    pieces = jnp.concatenate([pieces, jnp.zeros((EXTRA, W - S), F32)], 1).astype(BF16)
    for t in range(NT):
        send[t, S : 2 * S] = kv_part
        send[t, 2 * S : 3 * S] = out_slice
        send[t, 3 * S :] = pieces


def finish(got, stream, cot_stream, gain, inv_in, stream_out, stream_grad, kv_grad):
    grad = jnp.zeros((S, W), F32)
    lines = jnp.zeros((EXTRA, S), F32)
    for t in range(NT):
        grad += got[t, :S].astype(F32)
        lines += got[t, 3 * S :, :S].astype(F32)
        stream_out[:, t * W : (t + 1) * W] = got[t, 2 * S : 3 * S]
    share = GROUP * HS // W
    for j in range(NT // share):
        total = got[share * j, S : 2 * S].astype(F32)
        for i in range(1, share):
            total += got[share * j + i, S : 2 * S].astype(F32)
        kv_grad[:, j * W : (j + 1) * W] = total.astype(BF16)
    total = jnp.sum(lines, 0, keepdims=True)
    mean = jnp.broadcast_to(total, (S, S)).T[:, :1] * (1.0 / D)
    inv = inv_in[:, :1]
    grad = inv * (gain[...].astype(F32) * grad) - stream[...].astype(F32) * (inv * inv * inv) * mean
    stream_grad[...] = (cot_stream[...].astype(F32) + grad).astype(BF16)


def add_up(got, wq_grad, wo_grad):
    total = got[0].astype(F32)
    for z in range(1, ZH):
        total += got[z].astype(F32)
    wq_grad[...] = total[:, :W].astype(BF16)
    wo_grad[...] = total[:, W:].T.astype(BF16)


def per_device(
    stream_in, newer_partial, norm_gain, query_weight, keys_values, out_weight, cot_stream, cot_attn
):
    rank = lax.axis_index(TENSOR)
    gain = norm_gain.reshape(1, D)
    gain_own = lax.dynamic_slice_in_dim(gain, rank * W, W, 1)
    kv_own = lax.dynamic_slice_in_dim(keys_values, rank * W // HS // GROUP * 2 * HS, 2 * HS, 1)

    weights = call(
        pack_weights,
        arr(B, 2 * W),
        56,
        in_specs=[HBM] * 2,
        out_specs=VMEM,
        scratch_shapes=[pltpu.VMEM((W, B), BF16), pltpu.SemaphoreType.DMA((2,))],
    )(query_weight, out_weight)
    weights = lax.all_gather(weights, "zh", axis=0, tiled=True)
    weights = lax.all_gather(weights, "y", axis=0, tiled=True)

    send = call(pack_forward, arr(NT, 2 * S, W), 56)(stream_in, cot_attn)
    got = lax.all_to_all(send, TENSOR, 0, 0, tiled=True)
    normed, cot, normed_t, cot_t, inv = call(
        prepare, [arr(S, D), arr(S, D), arr(D, S), arr(D, S), arr(S, 128, of=F32)], 14
    )(got, gain)
    send = call(pack_partial, arr(NT, S, W), 56, in_specs=[VMEM, ANY])(newer_partial, inv)
    partials = lax.all_to_all(send, TENSOR, 0, 0, tiled=True)

    terms, kept = call(
        attend,
        [arr(D, 2 * W), arr(6, S, W)],
        46,
        flops=8 * S * D * W,
        in_specs=[VMEM] * 4 + [HBM, VMEM],
        out_specs=[HBM, VMEM],
        scratch_shapes=[
            pltpu.VMEM((D, 2 * W), BF16),
            pltpu.VMEM((D, 2 * W), BF16),
            pltpu.SemaphoreType.DMA((D // STEP,)),
            pltpu.SemaphoreType.DMA((D // STEP,)),
        ],
    )(normed, cot, normed_t, cot_t, weights, kv_own)

    terms = lax.psum_scatter(terms, "y", scatter_dimension=0, tiled=True)
    terms = lax.all_to_all(terms.reshape(ZH, B, 2 * W), "zh", 0, 0, tiled=True)
    wq_grad, wo_grad = call(add_up, [arr(B, W), arr(W, B)], 4)(terms)

    streams = pl.BlockSpec((NT, S, W), lambda i: (0, 0, 0))
    attn_partial, send = call(
        project,
        [arr(1, S, D), arr(NT, 3 * S + EXTRA, W)],
        56,
        flops=4 * S * D * W,
        grid=(1,),
        in_specs=[VMEM] * 2 + [streams] + [VMEM] * 3,
        out_specs=[VMEM, VMEM],
    )(kept, weights, got, gain, stream_in, partials)
    got = lax.all_to_all(send, TENSOR, 0, 0, tiled=True)
    stream_out, stream_grad, kv_grad = call(
        finish, [arr(S, D), arr(S, W), arr(*keys_values.shape)], 12
    )(got, stream_in, cot_stream, gain_own, inv)
    return (stream_out, attn_partial, stream_grad, kv_grad, wq_grad, wo_grad)


def solution(mesh):
    fine = Mesh(mesh.devices.reshape(ZH, Y, ZL, X, CORE), FSDP + TENSOR)
    return jax.shard_map(
        per_device,
        mesh=fine,
        in_specs=(
            P(FSDP, TENSOR),
            P(TENSOR, FSDP, None),
            P(),
            P(FSDP, TENSOR),
            P(FSDP, None),
            P(TENSOR, FSDP),
            P(FSDP, TENSOR),
            P(FSDP, TENSOR),
        ),
        out_specs=(
            P(FSDP, None),
            P(TENSOR, FSDP, None),
            P(FSDP, TENSOR),
            P(FSDP, None),
            P(FSDP, TENSOR),
            P(TENSOR, FSDP),
        ),
        check_vma=False,
    )
```

```python
import math

import jax
import jax.numpy as jnp
from jax import lax
from jax.experimental import pallas as pl
from jax.experimental.pallas import tpu as pltpu
from jax.sharding import Mesh, PartitionSpec as P

HS = 128
GROUP = 4
ZH, Y, ZL, X, CORE = 4, 8, 2, 4, 2
NT = ZL * X * CORE
NF = ZH * Y
TENSOR = ("zl", "x", "c")
FSDP = ("zh", "y")
S = 128
W = 256
D = NT * W
B = D // NF
EXTRA = 16
F32, BF16 = jnp.float32, jnp.bfloat16
HBM = pl.BlockSpec(memory_space=pltpu.HBM)
VMEM = pl.BlockSpec(memory_space=pltpu.VMEM)
STEP = 512


def call(body, outs, mib, flops=0, nbytes=0, **specs):
    return pl.pallas_call(
        body,
        out_shape=outs,
        compiler_params=pltpu.CompilerParams(vmem_limit_bytes=mib * 2**20),
        cost_estimate=pl.CostEstimate(flops=flops, bytes_accessed=nbytes, transcendentals=0),
        **specs,
    )


def arr(*dims, of=BF16):
    return jax.ShapeDtypeStruct(dims, of)


def place(f):
    return (f % Y) * ZH + f // Y


def nn(a, b):
    return lax.dot_general(a, b, (((1,), (0,)), ((), ())), preferred_element_type=F32)


def nt(a, b):
    return lax.dot_general(a, b, (((1,), (1,)), ((), ())), preferred_element_type=F32)


def flip(a):
    return a.astype(F32).T


def pack_weights(wq, wo, out, wo_held, sem):
    copies = [pltpu.make_async_copy(wo, wo_held, sem.at[0]), pltpu.make_async_copy(wq, out.at[:, :W], sem.at[1])]
    for copy in copies:
        copy.start()
    copies[0].wait()
    out[:, W:] = flip(wo_held[...]).astype(BF16)
    copies[1].wait()


def pack_forward(stream, cot, partial, out):
    for t in range(NT):
        out[t, :S] = stream[...]
        out[t, S : 2 * S] = cot[...]
        out[t, 2 * S :] = partial[0, :, t * W : (t + 1) * W]


def prepare(got, stream, gain, normed, cot, normed_t, cot_t, inv_out, out_slice):
    squares = jnp.zeros((S, 1), F32)
    pending = jnp.zeros((S, W), F32)
    for t in range(NT):
        block = got[t, :S].astype(F32)
        squares += jnp.sum(block * block, -1, keepdims=True)
        pending += got[t, 2 * S :].astype(F32)
    inv = lax.rsqrt(squares * (1.0 / D) + 1e-05)
    inv_out[...] = jnp.broadcast_to(inv, (S, 128))
    out_slice[...] = (stream[...].astype(F32) + pending).astype(BF16)
    for f in range(NF):
        t, half = f // 2, (f % 2) * B
        at = place(f) * B
        block = got[t, :S, half : half + B].astype(F32)
        block = block * inv * gain[:, f * B : (f + 1) * B].astype(F32)
        normed[:, at : at + B] = block.astype(BF16)
        normed_t[at : at + B] = block.T.astype(BF16)
        piece = got[t, S : 2 * S, half : half + B]
        cot[:, at : at + B] = piece
        cot_t[at : at + B] = flip(piece).astype(BF16)


def attend(
    normed_in, cot_in, normed_t_in, cot_t_in, weights, kv_in, terms, kept_out,
    normed, cot, normed_t, cot_t, w_held, t_held, kv, kept, sem, in_sem, t_sem,
):
    scale = 1.0 / math.sqrt(HS)
    chunks = [slice(i * STEP, (i + 1) * STEP) for i in range(D // STEP)]
    pairs = ((kv_in, kv), (normed_t_in, normed_t), (cot_t_in, cot_t))
    brought = [pltpu.make_async_copy(a, b, sem.at[i]) for i, (a, b) in enumerate(pairs)]
    arrived = [
        (
            pltpu.make_async_copy(normed_in.at[:, k], normed.at[:, k], in_sem.at[0, i]),
            pltpu.make_async_copy(cot_in.at[:, k], cot.at[:, k], in_sem.at[1, i]),
            pltpu.make_async_copy(weights.at[k], w_held.at[k], in_sem.at[2, i]),
        )
        for i, k in enumerate(chunks)
    ]
    for copies in arrived + [brought]:
        for copy in copies:
            copy.start()
    queries = jnp.zeros((S, W), F32)
    grads = jnp.zeros((S, W), F32)
    for copies, k in zip(arrived, chunks):
        for copy in copies:
            copy.wait()
        queries += nn(normed[:, k], w_held[k, :W])
        grads += nn(cot[:, k], w_held[k, W:])
    queries, grads = queries.astype(BF16), grads.astype(BF16)
    att_out, gq_out, low_out, gs_out = (kept.at[i] for i in range(4))
    kept[4] = queries
    kept[5] = grads
    brought[0].wait()
    keys, values = kv[:, :HS], kv[:, HS:]
    causal = lax.broadcasted_iota(jnp.int32, (S, S), 0) >= lax.broadcasted_iota(jnp.int32, (S, S), 1)
    for h in range(W // HS):
        at = slice(h * HS, (h + 1) * HS)
        q, g = queries[:, at], grads[:, at]
        scores = jnp.where(causal, nt(q, keys) * scale, -1e30)
        weight = jnp.exp(scores - jnp.max(scores, -1, keepdims=True))
        probs = weight / jnp.sum(weight, -1, keepdims=True)
        low = probs.astype(BF16)
        att = nn(low, values).astype(BF16)
        delta = jnp.sum(g.astype(F32) * att.astype(F32), -1, keepdims=True)
        gs = (probs * (nt(g, values) - delta) * scale).astype(BF16)
        gq_out[:, at] = nn(gs, keys).astype(BF16)
        att_out[:, at] = att
        low_out[:, at] = low
        gs_out[:, at] = gs
    att, gq = att_out[...], gq_out[...]
    leaving = [pltpu.make_async_copy(kept, kept_out, sem.at[3])]
    leaving[0].start()
    for copy in brought[1:]:
        copy.wait()
    for i, k in enumerate(chunks):
        t_held[k, :W] = nn(normed_t[k], gq).astype(BF16)
        t_held[k, W:] = nn(cot_t[k], att).astype(BF16)
        leaving.append(pltpu.make_async_copy(t_held.at[k], terms.at[k], t_sem.at[i]))
        leaving[-1].start()
    for copy in leaving:
        copy.wait()


def project(kept, weights, got, gain, out_slice, partial, send):
    att, gq, low, gs, q, g = (kept.at[i] for i in range(6))
    grad_keys = jnp.zeros((S, HS), F32)
    grad_values = jnp.zeros((S, HS), F32)
    for h in range(W // HS):
        at = slice(h * HS, (h + 1) * HS)
        grad_keys += nn(flip(gs[:, at]).astype(BF16), q[:, at])
        grad_values += nn(flip(low[:, at]).astype(BF16), g[:, at])
    kv_part = jnp.concatenate([grad_keys, grad_values], 1).astype(BF16)
    rows = jnp.zeros((S, 1), F32)
    for y in range(Y):
        k = slice(y * ZH * B, (y + 1) * ZH * B)
        out = nt(att[...], weights[k, W:]).astype(BF16)
        grad = nt(gq[...], weights[k, :W]).astype(BF16)
        for z in range(ZH):
            f = z * Y + y
            t, half = f // 2, (f % 2) * B
            block = grad[:, z * B : (z + 1) * B]
            partial[0, :, f * B : (f + 1) * B] = out[:, z * B : (z + 1) * B]
            send[t, :S, half : half + B] = block
            stream = got[t, :, half : half + B].astype(F32)
            scaled = gain[:, f * B : (f + 1) * B].astype(F32) * block.astype(F32)
            rows += jnp.sum(scaled * stream, -1, keepdims=True)
    across = jnp.broadcast_to(rows, (S, S)).T[:EXTRA]
    high = across.astype(BF16).astype(F32)
    middle = (across - high).astype(BF16).astype(F32)
    rest = across - high - middle
    line = lax.broadcasted_iota(jnp.int32, (EXTRA, S), 0)
    zero = jnp.zeros_like(rest)
    pieces = jnp.where(line == 0, high, jnp.where(line == 1, middle, jnp.where(line == 2, rest, zero)))
    pieces = jnp.concatenate([pieces, jnp.zeros((EXTRA, W - S), F32)], 1).astype(BF16)
    for t in range(NT):
        send[t, S : 2 * S] = kv_part
        send[t, 2 * S : 3 * S] = out_slice[...]
        send[t, 3 * S :] = pieces


def finish(got, stream, cot_stream, gain, inv_in, stream_out, stream_grad, kv_grad):
    grad = jnp.zeros((S, W), F32)
    lines = jnp.zeros((EXTRA, S), F32)
    for t in range(NT):
        grad += got[t, :S].astype(F32)
        lines += got[t, 3 * S :, :S].astype(F32)
        stream_out[:, t * W : (t + 1) * W] = got[t, 2 * S : 3 * S]
    share = GROUP * HS // W
    for j in range(NT // share):
        total = got[share * j, S : 2 * S].astype(F32)
        for i in range(1, share):
            total += got[share * j + i, S : 2 * S].astype(F32)
        kv_grad[:, j * W : (j + 1) * W] = total.astype(BF16)
    total = jnp.sum(lines, 0, keepdims=True)
    mean = jnp.broadcast_to(total, (S, S)).T[:, :1] * (1.0 / D)
    inv = inv_in[:, :1]
    grad = inv * (gain[...].astype(F32) * grad) - stream[...].astype(F32) * (inv * inv * inv) * mean
    stream_grad[...] = (cot_stream[...].astype(F32) + grad).astype(BF16)


def add_up(got, wq_grad, wo_grad):
    total = got[0].astype(F32)
    for z in range(1, ZH):
        total += got[z].astype(F32)
    wq_grad[...] = total[:, :W].astype(BF16)
    wo_grad[...] = total[:, W:].T.astype(BF16)


def per_device(
    stream_in, newer_partial, norm_gain, query_weight, keys_values, out_weight, cot_stream, cot_attn
):
    rank = lax.axis_index(TENSOR)
    gain = norm_gain.reshape(1, D)
    gain_own = lax.dynamic_slice_in_dim(gain, rank * W, W, 1)
    kv_own = lax.dynamic_slice_in_dim(keys_values, rank * W // HS // GROUP * 2 * HS, 2 * HS, 1)

    weights = call(
        pack_weights,
        arr(B, 2 * W),
        56,
        in_specs=[HBM] * 2,
        out_specs=VMEM,
        scratch_shapes=[pltpu.VMEM((W, B), BF16), pltpu.SemaphoreType.DMA((2,))],
    )(query_weight, out_weight)
    weights = lax.all_gather(weights, "zh", axis=0, tiled=True)
    weights = lax.all_gather(weights, "y", axis=0, tiled=True)

    send = call(pack_forward, arr(NT, 3 * S, W), 56)(stream_in, cot_attn, newer_partial)
    got = lax.all_to_all(send, TENSOR, 0, 0, tiled=True)
    normed, cot, normed_t, cot_t, inv, out_slice = call(
        prepare, [arr(S, D), arr(S, D), arr(D, S), arr(D, S), arr(S, 128, of=F32), arr(S, W)], 56
    )(got, stream_in, gain)

    terms, kept = call(
        attend,
        [arr(D, 2 * W), arr(6, S, W)],
        56,
        flops=8 * S * D * W,
        in_specs=[HBM] * 6,
        out_specs=[HBM, HBM],
        scratch_shapes=[
            pltpu.VMEM((S, D), BF16),
            pltpu.VMEM((S, D), BF16),
            pltpu.VMEM((D, S), BF16),
            pltpu.VMEM((D, S), BF16),
            pltpu.VMEM((D, 2 * W), BF16),
            pltpu.VMEM((D, 2 * W), BF16),
            pltpu.VMEM((S, 2 * HS), BF16),
            pltpu.VMEM((6, S, W), BF16),
            pltpu.SemaphoreType.DMA((4,)),
            pltpu.SemaphoreType.DMA((3, D // STEP)),
            pltpu.SemaphoreType.DMA((D // STEP,)),
        ],
    )(normed, cot, normed_t, cot_t, weights, kv_own)

    terms = lax.psum_scatter(terms, "y", scatter_dimension=0, tiled=True)
    terms = lax.all_to_all(terms.reshape(ZH, B, 2 * W), "zh", 0, 0, tiled=True)
    wq_grad, wo_grad = call(add_up, [arr(B, W), arr(W, B)], 4)(terms)

    streams = pl.BlockSpec((NT, S, W), lambda i: (0, 0, 0))
    attn_partial, send = call(
        project,
        [arr(1, S, D), arr(NT, 3 * S + EXTRA, W)],
        56,
        flops=4 * S * D * W,
        grid=(1,),
        in_specs=[VMEM] * 2 + [streams] + [VMEM] * 2,
        out_specs=[VMEM, VMEM],
    )(kept, weights, got, gain, out_slice)
    got = lax.all_to_all(send, TENSOR, 0, 0, tiled=True)
    stream_out, stream_grad, kv_grad = call(
        finish, [arr(S, D), arr(S, W), arr(*keys_values.shape)], 12
    )(got, stream_in, cot_stream, gain_own, inv)
    return (stream_out, attn_partial, stream_grad, kv_grad, wq_grad, wo_grad)


def solution(mesh):
    fine = Mesh(mesh.devices.reshape(ZH, Y, ZL, X, CORE), FSDP + TENSOR)
    return jax.shard_map(
        per_device,
        mesh=fine,
        in_specs=(
            P(FSDP, TENSOR),
            P(TENSOR, FSDP, None),
            P(),
            P(FSDP, TENSOR),
            P(FSDP, None),
            P(TENSOR, FSDP),
            P(FSDP, TENSOR),
            P(FSDP, TENSOR),
        ),
        out_specs=(
            P(FSDP, None),
            P(TENSOR, FSDP, None),
            P(FSDP, TENSOR),
            P(FSDP, None),
            P(FSDP, TENSOR),
            P(TENSOR, FSDP),
        ),
        check_vma=False,
    )
```

```python
import math

import jax
import jax.numpy as jnp
from jax import lax
from jax.experimental import pallas as pl
from jax.experimental.pallas import tpu as pltpu
from jax.sharding import Mesh, PartitionSpec as P

HS = 128
GROUP = 4
ZH, Y, ZL, X, CORE = 4, 8, 2, 4, 2
NT = ZL * X * CORE
NF = ZH * Y
TENSOR = ("zl", "x", "c")
FSDP = ("zh", "y")
S = 128
W = 256
D = NT * W
B = D // NF
EXTRA = 16
F32, BF16 = jnp.float32, jnp.bfloat16
HBM = pl.BlockSpec(memory_space=pltpu.HBM)
VMEM = pl.BlockSpec(memory_space=pltpu.VMEM)
STEP = 512


def call(body, outs, mib, flops=0, nbytes=0, **specs):
    return pl.pallas_call(
        body,
        out_shape=outs,
        compiler_params=pltpu.CompilerParams(vmem_limit_bytes=mib * 2**20),
        cost_estimate=pl.CostEstimate(flops=flops, bytes_accessed=nbytes, transcendentals=0),
        **specs,
    )


def arr(*dims, of=BF16):
    return jax.ShapeDtypeStruct(dims, of)


def place(f):
    return (f % Y) * ZH + f // Y


def nn(a, b):
    return lax.dot_general(a, b, (((1,), (0,)), ((), ())), preferred_element_type=F32)


def nt(a, b):
    return lax.dot_general(a, b, (((1,), (1,)), ((), ())), preferred_element_type=F32)


def flip(a):
    return a.astype(F32).T


def pack_weights(wq, wo, out, wo_held, sem):
    copies = [pltpu.make_async_copy(wo, wo_held, sem.at[0]), pltpu.make_async_copy(wq, out.at[:, :W], sem.at[1])]
    for copy in copies:
        copy.start()
    copies[0].wait()
    out[:, W:] = flip(wo_held[...]).astype(BF16)
    copies[1].wait()


def pack_forward(stream, cot, partial, out, sem):
    copies = []
    for t in range(NT):
        parts = (stream, cot, partial.at[0, :, t * W : (t + 1) * W])
        for i, part in enumerate(parts):
            copies.append(pltpu.make_async_copy(part, out.at[t, i * S : (i + 1) * S], sem.at[i, t]))
            copies[-1].start()
    for copy in copies:
        copy.wait()


def prepare(
    got_in, stream, gain, normed_out, cot_out, normed_t_out, cot_t_out, inv_out, out_slice,
    got, normed, cot, normed_t, cot_t, in_sem, cot_sem, normed_sem,
):
    arrived = [pltpu.make_async_copy(got_in.at[t], got.at[t], in_sem.at[t]) for t in range(NT)]
    for copy in arrived:
        copy.start()
    squares = jnp.zeros((S, 1), F32)
    pending = jnp.zeros((S, W), F32)
    for t in range(NT):
        arrived[t].wait()
        block = got[t, :S].astype(F32)
        squares += jnp.sum(block * block, -1, keepdims=True)
        pending += got[t, 2 * S :].astype(F32)
        for f in (2 * t, 2 * t + 1):
            at, half = place(f) * B, (f % 2) * B
            piece = got[t, S : 2 * S, half : half + B]
            cot[:, at : at + B] = piece
            cot_t[at : at + B] = flip(piece).astype(BF16)
    leaving = [
        pltpu.make_async_copy(cot, cot_out, cot_sem.at[0]),
        pltpu.make_async_copy(cot_t, cot_t_out, cot_sem.at[1]),
    ]
    for copy in leaving:
        copy.start()
    inv = lax.rsqrt(squares * (1.0 / D) + 1e-05)
    inv_out[...] = jnp.broadcast_to(inv, (S, 128))
    out_slice[...] = (stream[...].astype(F32) + pending).astype(BF16)
    for y in range(Y):
        for z in range(ZH):
            f = z * Y + y
            t, half, at = f // 2, (f % 2) * B, place(f) * B
            block = got[t, :S, half : half + B].astype(F32)
            block = block * inv * gain[:, f * B : (f + 1) * B].astype(F32)
            normed[:, at : at + B] = block.astype(BF16)
            normed_t[at : at + B] = block.T.astype(BF16)
        k = slice(y * ZH * B, (y + 1) * ZH * B)
        new = [
            pltpu.make_async_copy(normed.at[:, k], normed_out.at[:, k], normed_sem.at[0, y]),
            pltpu.make_async_copy(normed_t.at[k], normed_t_out.at[k], normed_sem.at[1, y]),
        ]
        for copy in new:
            copy.start()
        leaving += new
    for copy in leaving:
        copy.wait()


def attend(
    normed_in, cot_in, normed_t_in, cot_t_in, weights, kv_in, terms, kept_out,
    normed, cot, normed_t, cot_t, w_held, t_held, kv, kept, sem, in_sem, t_sem,
):
    scale = 1.0 / math.sqrt(HS)
    chunks = [slice(i * STEP, (i + 1) * STEP) for i in range(D // STEP)]
    pairs = ((kv_in, kv), (normed_t_in, normed_t), (cot_t_in, cot_t))
    brought = [pltpu.make_async_copy(a, b, sem.at[i]) for i, (a, b) in enumerate(pairs)]
    arrived = [
        (
            pltpu.make_async_copy(normed_in.at[:, k], normed.at[:, k], in_sem.at[0, i]),
            pltpu.make_async_copy(cot_in.at[:, k], cot.at[:, k], in_sem.at[1, i]),
            pltpu.make_async_copy(weights.at[k], w_held.at[k], in_sem.at[2, i]),
        )
        for i, k in enumerate(chunks)
    ]
    for copies in arrived + [brought]:
        for copy in copies:
            copy.start()
    queries = jnp.zeros((S, W), F32)
    grads = jnp.zeros((S, W), F32)
    for copies, k in zip(arrived, chunks):
        for copy in copies:
            copy.wait()
        queries += nn(normed[:, k], w_held[k, :W])
        grads += nn(cot[:, k], w_held[k, W:])
    queries, grads = queries.astype(BF16), grads.astype(BF16)
    att_out, gq_out, low_out, gs_out = (kept.at[i] for i in range(4))
    kept[4] = queries
    kept[5] = grads
    brought[0].wait()
    keys, values = kv[:, :HS], kv[:, HS:]
    causal = lax.broadcasted_iota(jnp.int32, (S, S), 0) >= lax.broadcasted_iota(jnp.int32, (S, S), 1)
    for h in range(W // HS):
        at = slice(h * HS, (h + 1) * HS)
        q, g = queries[:, at], grads[:, at]
        scores = jnp.where(causal, nt(q, keys) * scale, -1e30)
        weight = jnp.exp(scores - jnp.max(scores, -1, keepdims=True))
        probs = weight / jnp.sum(weight, -1, keepdims=True)
        low = probs.astype(BF16)
        att = nn(low, values).astype(BF16)
        delta = jnp.sum(g.astype(F32) * att.astype(F32), -1, keepdims=True)
        gs = (probs * (nt(g, values) - delta) * scale).astype(BF16)
        gq_out[:, at] = nn(gs, keys).astype(BF16)
        att_out[:, at] = att
        low_out[:, at] = low
        gs_out[:, at] = gs
    att, gq = att_out[...], gq_out[...]
    leaving = [pltpu.make_async_copy(kept, kept_out, sem.at[3])]
    leaving[0].start()
    for copy in brought[1:]:
        copy.wait()
    for i, k in enumerate(chunks):
        t_held[k, :W] = nn(normed_t[k], gq).astype(BF16)
        t_held[k, W:] = nn(cot_t[k], att).astype(BF16)
        leaving.append(pltpu.make_async_copy(t_held.at[k], terms.at[k], t_sem.at[i]))
        leaving[-1].start()
    for copy in leaving:
        copy.wait()


def project(kept, weights, got, gain, out_slice, partial, send):
    att, gq, low, gs, q, g = (kept.at[i] for i in range(6))
    grad_keys = jnp.zeros((S, HS), F32)
    grad_values = jnp.zeros((S, HS), F32)
    for h in range(W // HS):
        at = slice(h * HS, (h + 1) * HS)
        grad_keys += nn(flip(gs[:, at]).astype(BF16), q[:, at])
        grad_values += nn(flip(low[:, at]).astype(BF16), g[:, at])
    kv_part = jnp.concatenate([grad_keys, grad_values], 1).astype(BF16)
    rows = jnp.zeros((S, 1), F32)
    for y in range(Y):
        k = slice(y * ZH * B, (y + 1) * ZH * B)
        out = nt(att[...], weights[k, W:]).astype(BF16)
        grad = nt(gq[...], weights[k, :W]).astype(BF16)
        for z in range(ZH):
            f = z * Y + y
            t, half = f // 2, (f % 2) * B
            block = grad[:, z * B : (z + 1) * B]
            partial[0, :, f * B : (f + 1) * B] = out[:, z * B : (z + 1) * B]
            send[t, :S, half : half + B] = block
            stream = got[t, :, half : half + B].astype(F32)
            scaled = gain[:, f * B : (f + 1) * B].astype(F32) * block.astype(F32)
            rows += jnp.sum(scaled * stream, -1, keepdims=True)
    across = jnp.broadcast_to(rows, (S, S)).T[:EXTRA]
    high = across.astype(BF16).astype(F32)
    middle = (across - high).astype(BF16).astype(F32)
    rest = across - high - middle
    line = lax.broadcasted_iota(jnp.int32, (EXTRA, S), 0)
    zero = jnp.zeros_like(rest)
    pieces = jnp.where(line == 0, high, jnp.where(line == 1, middle, jnp.where(line == 2, rest, zero)))
    pieces = jnp.concatenate([pieces, jnp.zeros((EXTRA, W - S), F32)], 1).astype(BF16)
    for t in range(NT):
        send[t, S : 2 * S] = kv_part
        send[t, 2 * S : 3 * S] = out_slice[...]
        send[t, 3 * S :] = pieces


def finish(got, stream, cot_stream, gain, inv_in, stream_out, stream_grad, kv_grad):
    grad = jnp.zeros((S, W), F32)
    lines = jnp.zeros((EXTRA, S), F32)
    for t in range(NT):
        grad += got[t, :S].astype(F32)
        lines += got[t, 3 * S :, :S].astype(F32)
        stream_out[:, t * W : (t + 1) * W] = got[t, 2 * S : 3 * S]
    share = GROUP * HS // W
    for j in range(NT // share):
        total = got[share * j, S : 2 * S].astype(F32)
        for i in range(1, share):
            total += got[share * j + i, S : 2 * S].astype(F32)
        kv_grad[:, j * W : (j + 1) * W] = total.astype(BF16)
    total = jnp.sum(lines, 0, keepdims=True)
    mean = jnp.broadcast_to(total, (S, S)).T[:, :1] * (1.0 / D)
    inv = inv_in[:, :1]
    grad = inv * (gain[...].astype(F32) * grad) - stream[...].astype(F32) * (inv * inv * inv) * mean
    stream_grad[...] = (cot_stream[...].astype(F32) + grad).astype(BF16)


def add_up(got, wq_grad, wo_grad):
    total = got[0].astype(F32)
    for z in range(1, ZH):
        total += got[z].astype(F32)
    wq_grad[...] = total[:, :W].astype(BF16)
    wo_grad[...] = total[:, W:].T.astype(BF16)


def per_device(
    stream_in, newer_partial, norm_gain, query_weight, keys_values, out_weight, cot_stream, cot_attn
):
    rank = lax.axis_index(TENSOR)
    gain = norm_gain.reshape(1, D)
    gain_own = lax.dynamic_slice_in_dim(gain, rank * W, W, 1)
    kv_own = lax.dynamic_slice_in_dim(keys_values, rank * W // HS // GROUP * 2 * HS, 2 * HS, 1)

    weights = call(
        pack_weights,
        arr(B, 2 * W),
        56,
        in_specs=[HBM] * 2,
        out_specs=VMEM,
        scratch_shapes=[pltpu.VMEM((W, B), BF16), pltpu.SemaphoreType.DMA((2,))],
    )(query_weight, out_weight)
    weights = lax.all_gather(weights, "zh", axis=0, tiled=True)
    weights = lax.all_gather(weights, "y", axis=0, tiled=True)

    send = call(
        pack_forward,
        arr(NT, 3 * S, W),
        56,
        in_specs=[VMEM, VMEM, HBM],
        out_specs=HBM,
        scratch_shapes=[pltpu.SemaphoreType.DMA((3, NT))],
    )(stream_in, cot_attn, newer_partial)
    got = lax.all_to_all(send, TENSOR, 0, 0, tiled=True)
    normed, cot, normed_t, cot_t, inv, out_slice = call(
        prepare,
        [arr(S, D), arr(S, D), arr(D, S), arr(D, S), arr(S, 128, of=F32), arr(S, W)],
        56,
        in_specs=[HBM, VMEM, VMEM],
        out_specs=[HBM] * 4 + [VMEM] * 2,
        scratch_shapes=[
            pltpu.VMEM((NT, 3 * S, W), BF16),
            pltpu.VMEM((S, D), BF16),
            pltpu.VMEM((S, D), BF16),
            pltpu.VMEM((D, S), BF16),
            pltpu.VMEM((D, S), BF16),
            pltpu.SemaphoreType.DMA((NT,)),
            pltpu.SemaphoreType.DMA((2,)),
            pltpu.SemaphoreType.DMA((2, Y)),
        ],
    )(got, stream_in, gain)

    terms, kept = call(
        attend,
        [arr(D, 2 * W), arr(6, S, W)],
        56,
        flops=8 * S * D * W,
        in_specs=[HBM] * 6,
        out_specs=[HBM, HBM],
        scratch_shapes=[
            pltpu.VMEM((S, D), BF16),
            pltpu.VMEM((S, D), BF16),
            pltpu.VMEM((D, S), BF16),
            pltpu.VMEM((D, S), BF16),
            pltpu.VMEM((D, 2 * W), BF16),
            pltpu.VMEM((D, 2 * W), BF16),
            pltpu.VMEM((S, 2 * HS), BF16),
            pltpu.VMEM((6, S, W), BF16),
            pltpu.SemaphoreType.DMA((4,)),
            pltpu.SemaphoreType.DMA((3, D // STEP)),
            pltpu.SemaphoreType.DMA((D // STEP,)),
        ],
    )(normed, cot, normed_t, cot_t, weights, kv_own)

    terms = lax.psum_scatter(terms, "y", scatter_dimension=0, tiled=True)
    terms = lax.all_to_all(terms.reshape(ZH, B, 2 * W), "zh", 0, 0, tiled=True)
    wq_grad, wo_grad = call(add_up, [arr(B, W), arr(W, B)], 4)(terms)

    streams = pl.BlockSpec((NT, S, W), lambda i: (0, 0, 0))
    attn_partial, send = call(
        project,
        [arr(1, S, D), arr(NT, 3 * S + EXTRA, W)],
        56,
        flops=4 * S * D * W,
        grid=(1,),
        in_specs=[VMEM] * 2 + [streams] + [VMEM] * 2,
        out_specs=[VMEM, VMEM],
    )(kept, weights, got, gain, out_slice)
    got = lax.all_to_all(send, TENSOR, 0, 0, tiled=True)
    stream_out, stream_grad, kv_grad = call(
        finish, [arr(S, D), arr(S, W), arr(*keys_values.shape)], 12
    )(got, stream_in, cot_stream, gain_own, inv)
    return (stream_out, attn_partial, stream_grad, kv_grad, wq_grad, wo_grad)


def solution(mesh):
    fine = Mesh(mesh.devices.reshape(ZH, Y, ZL, X, CORE), FSDP + TENSOR)
    return jax.shard_map(
        per_device,
        mesh=fine,
        in_specs=(
            P(FSDP, TENSOR),
            P(TENSOR, FSDP, None),
            P(),
            P(FSDP, TENSOR),
            P(FSDP, None),
            P(TENSOR, FSDP),
            P(FSDP, TENSOR),
            P(FSDP, TENSOR),
        ),
        out_specs=(
            P(FSDP, None),
            P(TENSOR, FSDP, None),
            P(FSDP, TENSOR),
            P(FSDP, None),
            P(FSDP, TENSOR),
            P(TENSOR, FSDP),
        ),
        check_vma=False,
    )
```

```python
import math

import jax
import jax.numpy as jnp
from jax import lax
from jax.experimental import pallas as pl
from jax.experimental.pallas import tpu as pltpu
from jax.sharding import Mesh, PartitionSpec as P

HS = 128
GROUP = 4
ZH, Y, ZL, X, CORE = 4, 8, 2, 4, 2
NT = ZL * X * CORE
NF = ZH * Y
TENSOR = ("zl", "x", "c")
FSDP = ("zh", "y")
S = 128
W = 256
D = NT * W
B = D // NF
EXTRA = 16
F32, BF16 = jnp.float32, jnp.bfloat16
HBM = pl.BlockSpec(memory_space=pltpu.HBM)
VMEM = pl.BlockSpec(memory_space=pltpu.VMEM)
STEP = 512


def call(body, outs, mib, flops=0, nbytes=0, **specs):
    return pl.pallas_call(
        body,
        out_shape=outs,
        compiler_params=pltpu.CompilerParams(vmem_limit_bytes=mib * 2**20),
        cost_estimate=pl.CostEstimate(flops=flops, bytes_accessed=nbytes, transcendentals=0),
        **specs,
    )


def arr(*dims, of=BF16):
    return jax.ShapeDtypeStruct(dims, of)


def place(f):
    return (f % Y) * ZH + f // Y


def nn(a, b):
    return lax.dot_general(a, b, (((1,), (0,)), ((), ())), preferred_element_type=F32)


def nt(a, b):
    return lax.dot_general(a, b, (((1,), (1,)), ((), ())), preferred_element_type=F32)


def flip(a):
    return a.astype(F32).T


def pack_weights(wq, wo, out, wo_held, sem):
    copies = [pltpu.make_async_copy(wo, wo_held, sem.at[0]), pltpu.make_async_copy(wq, out.at[:, :W], sem.at[1])]
    for copy in copies:
        copy.start()
    copies[0].wait()
    out[:, W:] = flip(wo_held[...]).astype(BF16)
    copies[1].wait()


def pack_forward(stream, cot, partial, out):
    for t in range(out.shape[0]):
        out[t, :S] = stream[...]
        out[t, S : 2 * S] = cot[...]
        out[t, 2 * S :] = partial[0, :, t * W : (t + 1) * W]


def prepare(got, gain, normed, cot, normed_t, cot_t, inv_out):
    squares = jnp.zeros((S, 1), F32)
    for t in range(NT):
        block = got[t, :S].astype(F32)
        squares += jnp.sum(block * block, -1, keepdims=True)
    inv = lax.rsqrt(squares * (1.0 / D) + 1e-05)
    inv_out[...] = jnp.broadcast_to(inv, (S, 128))
    for f in range(NF):
        t, half = f // 2, (f % 2) * B
        at = place(f) * B
        block = got[t, :S, half : half + B].astype(F32)
        block = block * inv * gain[:, f * B : (f + 1) * B].astype(F32)
        normed[:, at : at + B] = block.astype(BF16)
        normed_t[at : at + B] = block.T.astype(BF16)
        piece = got[t, S : 2 * S, half : half + B]
        cot[:, at : at + B] = piece
        cot_t[at : at + B] = flip(piece).astype(BF16)


def attend(
    normed_in, cot_in, normed_t_in, cot_t_in, weights, kv_in, terms, kept_out,
    normed, cot, normed_t, cot_t, w_held, t_held, kv, kept, sem, in_sem, t_sem,
):
    scale = 1.0 / math.sqrt(HS)
    chunks = [slice(i * STEP, (i + 1) * STEP) for i in range(D // STEP)]
    pairs = ((kv_in, kv), (normed_t_in, normed_t), (cot_t_in, cot_t))
    brought = [pltpu.make_async_copy(a, b, sem.at[i]) for i, (a, b) in enumerate(pairs)]
    arrived = [
        (
            pltpu.make_async_copy(normed_in.at[:, k], normed.at[:, k], in_sem.at[0, i]),
            pltpu.make_async_copy(cot_in.at[:, k], cot.at[:, k], in_sem.at[1, i]),
            pltpu.make_async_copy(weights.at[k], w_held.at[k], in_sem.at[2, i]),
        )
        for i, k in enumerate(chunks)
    ]
    for copies in arrived + [brought]:
        for copy in copies:
            copy.start()
    queries = jnp.zeros((S, W), F32)
    grads = jnp.zeros((S, W), F32)
    for copies, k in zip(arrived, chunks):
        for copy in copies:
            copy.wait()
        queries += nn(normed[:, k], w_held[k, :W])
        grads += nn(cot[:, k], w_held[k, W:])
    queries, grads = queries.astype(BF16), grads.astype(BF16)
    att_out, gq_out, low_out, gs_out = (kept.at[i] for i in range(4))
    kept[4] = queries
    kept[5] = grads
    brought[0].wait()
    keys, values = kv[:, :HS], kv[:, HS:]
    causal = lax.broadcasted_iota(jnp.int32, (S, S), 0) >= lax.broadcasted_iota(jnp.int32, (S, S), 1)
    for h in range(W // HS):
        at = slice(h * HS, (h + 1) * HS)
        q, g = queries[:, at], grads[:, at]
        scores = jnp.where(causal, nt(q, keys) * scale, -1e30)
        weight = jnp.exp(scores - jnp.max(scores, -1, keepdims=True))
        probs = weight / jnp.sum(weight, -1, keepdims=True)
        low = probs.astype(BF16)
        att = nn(low, values).astype(BF16)
        delta = jnp.sum(g.astype(F32) * att.astype(F32), -1, keepdims=True)
        gs = (probs * (nt(g, values) - delta) * scale).astype(BF16)
        gq_out[:, at] = nn(gs, keys).astype(BF16)
        att_out[:, at] = att
        low_out[:, at] = low
        gs_out[:, at] = gs
    att, gq = att_out[...], gq_out[...]
    leaving = [pltpu.make_async_copy(kept, kept_out, sem.at[3])]
    leaving[0].start()
    for copy in brought[1:]:
        copy.wait()
    for i, k in enumerate(chunks):
        t_held[k, :W] = nn(normed_t[k], gq).astype(BF16)
        t_held[k, W:] = nn(cot_t[k], att).astype(BF16)
        leaving.append(pltpu.make_async_copy(t_held.at[k], terms.at[k], t_sem.at[i]))
        leaving[-1].start()
    for copy in leaving:
        copy.wait()


def project(kept, weights, got, pending_in, gain, own, partial, send):
    pending = jnp.zeros((S, W), F32)
    for t in range(NT):
        pending += pending_in[t].astype(F32)
    out_slice = (own[...].astype(F32) + pending).astype(BF16)
    att, gq, low, gs, q, g = (kept.at[i] for i in range(6))
    grad_keys = jnp.zeros((S, HS), F32)
    grad_values = jnp.zeros((S, HS), F32)
    for h in range(W // HS):
        at = slice(h * HS, (h + 1) * HS)
        grad_keys += nn(flip(gs[:, at]).astype(BF16), q[:, at])
        grad_values += nn(flip(low[:, at]).astype(BF16), g[:, at])
    kv_part = jnp.concatenate([grad_keys, grad_values], 1).astype(BF16)
    rows = jnp.zeros((S, 1), F32)
    for y in range(Y):
        k = slice(y * ZH * B, (y + 1) * ZH * B)
        out = nt(att[...], weights[k, W:]).astype(BF16)
        grad = nt(gq[...], weights[k, :W]).astype(BF16)
        for z in range(ZH):
            f = z * Y + y
            t, half = f // 2, (f % 2) * B
            block = grad[:, z * B : (z + 1) * B]
            partial[0, :, f * B : (f + 1) * B] = out[:, z * B : (z + 1) * B]
            send[t, :S, half : half + B] = block
            stream = got[t, :, half : half + B].astype(F32)
            scaled = gain[:, f * B : (f + 1) * B].astype(F32) * block.astype(F32)
            rows += jnp.sum(scaled * stream, -1, keepdims=True)
    across = jnp.broadcast_to(rows, (S, S)).T[:EXTRA]
    high = across.astype(BF16).astype(F32)
    middle = (across - high).astype(BF16).astype(F32)
    rest = across - high - middle
    line = lax.broadcasted_iota(jnp.int32, (EXTRA, S), 0)
    zero = jnp.zeros_like(rest)
    pieces = jnp.where(line == 0, high, jnp.where(line == 1, middle, jnp.where(line == 2, rest, zero)))
    pieces = jnp.concatenate([pieces, jnp.zeros((EXTRA, W - S), F32)], 1).astype(BF16)
    for t in range(NT):
        send[t, S : 2 * S] = kv_part
        send[t, 2 * S : 3 * S] = out_slice
        send[t, 3 * S :] = pieces


def finish(got, stream, cot_stream, gain, inv_in, stream_out, stream_grad, kv_grad):
    grad = jnp.zeros((S, W), F32)
    lines = jnp.zeros((EXTRA, S), F32)
    for t in range(NT):
        grad += got[t, :S].astype(F32)
        lines += got[t, 3 * S :, :S].astype(F32)
        stream_out[:, t * W : (t + 1) * W] = got[t, 2 * S : 3 * S]
    share = GROUP * HS // W
    for j in range(NT // share):
        total = got[share * j, S : 2 * S].astype(F32)
        for i in range(1, share):
            total += got[share * j + i, S : 2 * S].astype(F32)
        kv_grad[:, j * W : (j + 1) * W] = total.astype(BF16)
    total = jnp.sum(lines, 0, keepdims=True)
    mean = jnp.broadcast_to(total, (S, S)).T[:, :1] * (1.0 / D)
    inv = inv_in[:, :1]
    grad = inv * (gain[...].astype(F32) * grad) - stream[...].astype(F32) * (inv * inv * inv) * mean
    stream_grad[...] = (cot_stream[...].astype(F32) + grad).astype(BF16)


def add_up(got, wq_grad, wo_grad):
    total = got[0].astype(F32)
    for z in range(1, ZH):
        total += got[z].astype(F32)
    wq_grad[...] = total[:, :W].astype(BF16)
    wo_grad[...] = total[:, W:].T.astype(BF16)


def per_device(
    stream_in, newer_partial, norm_gain, query_weight, keys_values, out_weight, cot_stream, cot_attn
):
    rank = lax.axis_index(TENSOR)
    gain = norm_gain.reshape(1, D)
    gain_own = lax.dynamic_slice_in_dim(gain, rank * W, W, 1)
    kv_own = lax.dynamic_slice_in_dim(keys_values, rank * W // HS // GROUP * 2 * HS, 2 * HS, 1)

    weights = call(
        pack_weights,
        arr(B, 2 * W),
        56,
        in_specs=[HBM] * 2,
        out_specs=VMEM,
        scratch_shapes=[pltpu.VMEM((W, B), BF16), pltpu.SemaphoreType.DMA((2,))],
    )(query_weight, out_weight)
    weights = lax.all_gather(weights, "zh", axis=0, tiled=True)
    weights = lax.all_gather(weights, "y", axis=0, tiled=True)

    whole, steps = pl.BlockSpec((S, W), lambda i: (0, 0)), 4
    send = call(
        pack_forward,
        arr(NT, 3 * S, W),
        56,
        grid=(steps,),
        in_specs=[whole, whole, pl.BlockSpec((1, S, D // steps), lambda i: (0, 0, i))],
        out_specs=pl.BlockSpec((NT // steps, 3 * S, W), lambda i: (i, 0, 0)),
    )(stream_in, cot_attn, newer_partial)
    got = lax.all_to_all(send, TENSOR, 0, 0, tiled=True)
    normed, cot, normed_t, cot_t, inv = call(
        prepare,
        [arr(S, D), arr(S, D), arr(D, S), arr(D, S), arr(S, 128, of=F32)],
        56,
        grid=(1,),
        in_specs=[pl.BlockSpec((NT, 2 * S, W), lambda i: (0, 0, 0)), VMEM],
        out_specs=[VMEM] * 5,
    )(got, gain)

    terms, kept = call(
        attend,
        [arr(D, 2 * W), arr(6, S, W)],
        56,
        flops=8 * S * D * W,
        in_specs=[HBM] * 6,
        out_specs=[HBM, HBM],
        scratch_shapes=[
            pltpu.VMEM((S, D), BF16),
            pltpu.VMEM((S, D), BF16),
            pltpu.VMEM((D, S), BF16),
            pltpu.VMEM((D, S), BF16),
            pltpu.VMEM((D, 2 * W), BF16),
            pltpu.VMEM((D, 2 * W), BF16),
            pltpu.VMEM((S, 2 * HS), BF16),
            pltpu.VMEM((6, S, W), BF16),
            pltpu.SemaphoreType.DMA((4,)),
            pltpu.SemaphoreType.DMA((3, D // STEP)),
            pltpu.SemaphoreType.DMA((D // STEP,)),
        ],
    )(normed, cot, normed_t, cot_t, weights, kv_own)

    terms = lax.psum_scatter(terms, "y", scatter_dimension=0, tiled=True)
    terms = lax.all_to_all(terms.reshape(ZH, B, 2 * W), "zh", 0, 0, tiled=True)
    wq_grad, wo_grad = call(add_up, [arr(B, W), arr(W, B)], 4)(terms)

    streams = pl.BlockSpec((NT, S, W), lambda i: (0, 0, 0))
    pieces = pl.BlockSpec((NT, S, W), lambda i: (0, 2, 0))
    attn_partial, send = call(
        project,
        [arr(1, S, D), arr(NT, 3 * S + EXTRA, W)],
        56,
        flops=4 * S * D * W,
        grid=(1,),
        in_specs=[VMEM] * 2 + [streams, pieces] + [VMEM] * 2,
        out_specs=[VMEM, VMEM],
    )(kept, weights, got, got, gain, stream_in)
    got = lax.all_to_all(send, TENSOR, 0, 0, tiled=True)
    stream_out, stream_grad, kv_grad = call(
        finish, [arr(S, D), arr(S, W), arr(*keys_values.shape)], 12
    )(got, stream_in, cot_stream, gain_own, inv)
    return (stream_out, attn_partial, stream_grad, kv_grad, wq_grad, wo_grad)


def solution(mesh):
    fine = Mesh(mesh.devices.reshape(ZH, Y, ZL, X, CORE), FSDP + TENSOR)
    return jax.shard_map(
        per_device,
        mesh=fine,
        in_specs=(
            P(FSDP, TENSOR),
            P(TENSOR, FSDP, None),
            P(),
            P(FSDP, TENSOR),
            P(FSDP, None),
            P(TENSOR, FSDP),
            P(FSDP, TENSOR),
            P(FSDP, TENSOR),
        ),
        out_specs=(
            P(FSDP, None),
            P(TENSOR, FSDP, None),
            P(FSDP, TENSOR),
            P(FSDP, None),
            P(FSDP, TENSOR),
            P(TENSOR, FSDP),
        ),
        check_vma=False,
    )
```

```python
import math

import jax
import jax.numpy as jnp
from jax import lax
from jax.experimental import pallas as pl
from jax.experimental.pallas import tpu as pltpu
from jax.sharding import Mesh, PartitionSpec as P

HS = 128
GROUP = 4
ZH, Y, ZL, X, CORE = 4, 8, 2, 4, 2
NT = ZL * X * CORE
NF = ZH * Y
TENSOR = ("zl", "x", "c")
FSDP = ("zh", "y")
S = 128
W = 256
D = NT * W
B = D // NF
EXTRA = 16
F32, BF16 = jnp.float32, jnp.bfloat16
HBM = pl.BlockSpec(memory_space=pltpu.HBM)
VMEM = pl.BlockSpec(memory_space=pltpu.VMEM)
STEP = 512


def call(body, outs, mib, flops=0, nbytes=0, **specs):
    return pl.pallas_call(
        body,
        out_shape=outs,
        compiler_params=pltpu.CompilerParams(vmem_limit_bytes=mib * 2**20),
        cost_estimate=pl.CostEstimate(flops=flops, bytes_accessed=nbytes, transcendentals=0),
        **specs,
    )


def arr(*dims, of=BF16):
    return jax.ShapeDtypeStruct(dims, of)


def place(f):
    return (f % Y) * ZH + f // Y


def nn(a, b):
    return lax.dot_general(a, b, (((1,), (0,)), ((), ())), preferred_element_type=F32)


def nt(a, b):
    return lax.dot_general(a, b, (((1,), (1,)), ((), ())), preferred_element_type=F32)


def flip(a):
    return a.astype(F32).T


def pack_weights(wq, wo, out, wo_held, sem):
    copies = [pltpu.make_async_copy(wo, wo_held, sem.at[0]), pltpu.make_async_copy(wq, out.at[:, :W], sem.at[1])]
    for copy in copies:
        copy.start()
    copies[0].wait()
    out[:, W:] = flip(wo_held[...]).astype(BF16)
    copies[1].wait()


def pack_forward(stream, cot, partial, out):
    for t in range(NT):
        out[t, :S] = stream[...]
        out[t, S : 2 * S] = cot[...]
        out[t, 2 * S :] = partial[0, :, t * W : (t + 1) * W]


def prepare(got, stream, gain, normed, cot, normed_t, cot_t, inv_out, out_slice):
    squares = jnp.zeros((S, 1), F32)
    pending = jnp.zeros((S, W), F32)
    for t in range(NT):
        block = got[t, :S].astype(F32)
        squares += jnp.sum(block * block, -1, keepdims=True)
        pending += got[t, 2 * S :].astype(F32)
    inv = lax.rsqrt(squares * (1.0 / D) + 1e-05)
    inv_out[...] = jnp.broadcast_to(inv, (S, 128))
    out_slice[...] = (stream[...].astype(F32) + pending).astype(BF16)
    for f in range(NF):
        t, half = f // 2, (f % 2) * B
        at = place(f) * B
        block = got[t, :S, half : half + B].astype(F32)
        block = block * inv * gain[:, f * B : (f + 1) * B].astype(F32)
        normed[:, at : at + B] = block.astype(BF16)
        normed_t[at : at + B] = block.T.astype(BF16)
        piece = got[t, S : 2 * S, half : half + B]
        cot[:, at : at + B] = piece
        cot_t[at : at + B] = flip(piece).astype(BF16)


def attend(
    normed_in, cot_in, normed_t_in, cot_t_in, weights, kv_in, terms, kept_out,
    normed, cot, normed_t, cot_t, w_held, t_held, kv, kept, sem, in_sem, t_sem,
):
    scale = 1.0 / math.sqrt(HS)
    chunks = [slice(i * STEP, (i + 1) * STEP) for i in range(D // STEP)]
    pairs = ((kv_in, kv), (normed_t_in, normed_t), (cot_t_in, cot_t))
    brought = [pltpu.make_async_copy(a, b, sem.at[i]) for i, (a, b) in enumerate(pairs)]
    arrived = [
        (
            pltpu.make_async_copy(normed_in.at[:, k], normed.at[:, k], in_sem.at[0, i]),
            pltpu.make_async_copy(cot_in.at[:, k], cot.at[:, k], in_sem.at[1, i]),
            pltpu.make_async_copy(weights.at[k], w_held.at[k], in_sem.at[2, i]),
        )
        for i, k in enumerate(chunks)
    ]
    for copies in arrived + [brought]:
        for copy in copies:
            copy.start()
    queries = jnp.zeros((S, W), F32)
    grads = jnp.zeros((S, W), F32)
    for copies, k in zip(arrived, chunks):
        for copy in copies:
            copy.wait()
        queries += nn(normed[:, k], w_held[k, :W])
        grads += nn(cot[:, k], w_held[k, W:])
    queries, grads = queries.astype(BF16), grads.astype(BF16)
    att_out, gq_out, low_out, gs_out = (kept.at[i] for i in range(4))
    kept[4] = queries
    kept[5] = grads
    brought[0].wait()
    keys, values = kv[:, :HS], kv[:, HS:]
    causal = lax.broadcasted_iota(jnp.int32, (S, S), 0) >= lax.broadcasted_iota(jnp.int32, (S, S), 1)
    for h in range(W // HS):
        at = slice(h * HS, (h + 1) * HS)
        q, g = queries[:, at], grads[:, at]
        scores = jnp.where(causal, nt(q, keys) * scale, -1e30)
        weight = jnp.exp(scores - jnp.max(scores, -1, keepdims=True))
        probs = weight / jnp.sum(weight, -1, keepdims=True)
        low = probs.astype(BF16)
        att = nn(low, values).astype(BF16)
        delta = jnp.sum(g.astype(F32) * att.astype(F32), -1, keepdims=True)
        gs = (probs * (nt(g, values) - delta) * scale).astype(BF16)
        gq_out[:, at] = nn(gs, keys).astype(BF16)
        att_out[:, at] = att
        low_out[:, at] = low
        gs_out[:, at] = gs
    att, gq = att_out[...], gq_out[...]
    leaving = [pltpu.make_async_copy(kept, kept_out, sem.at[3])]
    leaving[0].start()
    for copy in brought[1:]:
        copy.wait()
    for i, k in enumerate(chunks):
        t_held[k, :W] = nn(normed_t[k], gq).astype(BF16)
        t_held[k, W:] = nn(cot_t[k], att).astype(BF16)
        leaving.append(pltpu.make_async_copy(t_held.at[k], terms.at[k], t_sem.at[i]))
        leaving[-1].start()
    for copy in leaving:
        copy.wait()


def project(kept, weights, got, gain, out_slice, partial, send):
    att, gq, low, gs, q, g = (kept.at[i] for i in range(6))
    grad_keys = jnp.zeros((S, HS), F32)
    grad_values = jnp.zeros((S, HS), F32)
    for h in range(W // HS):
        at = slice(h * HS, (h + 1) * HS)
        grad_keys += nn(flip(gs[:, at]).astype(BF16), q[:, at])
        grad_values += nn(flip(low[:, at]).astype(BF16), g[:, at])
    kv_part = jnp.concatenate([grad_keys, grad_values], 1).astype(BF16)
    rows = jnp.zeros((S, 1), F32)
    for y in range(Y):
        k = slice(y * ZH * B, (y + 1) * ZH * B)
        out = nt(att[...], weights[k, W:]).astype(BF16)
        grad = nt(gq[...], weights[k, :W]).astype(BF16)
        for z in range(ZH):
            f = z * Y + y
            t, half = f // 2, (f % 2) * B
            block = grad[:, z * B : (z + 1) * B]
            partial[0, :, f * B : (f + 1) * B] = out[:, z * B : (z + 1) * B]
            send[t, :S, half : half + B] = block
            stream = got[t, :, half : half + B].astype(F32)
            scaled = gain[:, f * B : (f + 1) * B].astype(F32) * block.astype(F32)
            rows += jnp.sum(scaled * stream, -1, keepdims=True)
    across = jnp.broadcast_to(rows, (S, S)).T[:EXTRA]
    high = across.astype(BF16).astype(F32)
    middle = (across - high).astype(BF16).astype(F32)
    rest = across - high - middle
    line = lax.broadcasted_iota(jnp.int32, (EXTRA, S), 0)
    zero = jnp.zeros_like(rest)
    pieces = jnp.where(line == 0, high, jnp.where(line == 1, middle, jnp.where(line == 2, rest, zero)))
    pieces = jnp.concatenate([pieces, jnp.zeros((EXTRA, W - S), F32)], 1).astype(BF16)
    for t in range(NT):
        send[t, S : 2 * S] = kv_part
        send[t, 2 * S : 3 * S] = out_slice[...]
        send[t, 3 * S :] = pieces


def finish(got, stream, cot_stream, gain, inv_in, stream_out, stream_grad, kv_grad):
    grad = jnp.zeros((S, W), F32)
    lines = jnp.zeros((EXTRA, S), F32)
    for t in range(NT):
        grad += got[t, :S].astype(F32)
        lines += got[t, 3 * S :, :S].astype(F32)
        stream_out[:, t * W : (t + 1) * W] = got[t, 2 * S : 3 * S]
    share = GROUP * HS // W
    for j in range(NT // share):
        total = got[share * j, S : 2 * S].astype(F32)
        for i in range(1, share):
            total += got[share * j + i, S : 2 * S].astype(F32)
        kv_grad[:, j * W : (j + 1) * W] = total.astype(BF16)
    total = jnp.sum(lines, 0, keepdims=True)
    mean = jnp.broadcast_to(total, (S, S)).T[:, :1] * (1.0 / D)
    inv = inv_in[:, :1]
    grad = inv * (gain[...].astype(F32) * grad) - stream[...].astype(F32) * (inv * inv * inv) * mean
    stream_grad[...] = (cot_stream[...].astype(F32) + grad).astype(BF16)


def add_up(own, first, second, third, wq_grad, wo_grad):
    total = own[...].astype(F32)
    for got in (first, second, third):
        total += got[...].astype(F32)
    wq_grad[...] = total[:, :W].astype(BF16)
    wo_grad[...] = total[:, W:].T.astype(BF16)


def per_device(
    stream_in, newer_partial, norm_gain, query_weight, keys_values, out_weight, cot_stream, cot_attn
):
    rank = lax.axis_index(TENSOR)
    gain = norm_gain.reshape(1, D)
    gain_own = lax.dynamic_slice_in_dim(gain, rank * W, W, 1)
    kv_own = lax.dynamic_slice_in_dim(keys_values, rank * W // HS // GROUP * 2 * HS, 2 * HS, 1)

    weights = call(
        pack_weights,
        arr(B, 2 * W),
        56,
        in_specs=[HBM] * 2,
        out_specs=VMEM,
        scratch_shapes=[pltpu.VMEM((W, B), BF16), pltpu.SemaphoreType.DMA((2,))],
    )(query_weight, out_weight)
    weights = lax.all_gather(weights, "zh", axis=0, tiled=True)
    weights = lax.all_gather(weights, "y", axis=0, tiled=True)

    send = call(pack_forward, arr(NT, 3 * S, W), 56)(stream_in, cot_attn, newer_partial)
    got = lax.all_to_all(send, TENSOR, 0, 0, tiled=True)
    normed, cot, normed_t, cot_t, inv, out_slice = call(
        prepare, [arr(S, D), arr(S, D), arr(D, S), arr(D, S), arr(S, 128, of=F32), arr(S, W)], 56
    )(got, stream_in, gain)

    terms, kept = call(
        attend,
        [arr(D, 2 * W), arr(6, S, W)],
        56,
        flops=8 * S * D * W,
        in_specs=[HBM] * 6,
        out_specs=[HBM, HBM],
        scratch_shapes=[
            pltpu.VMEM((S, D), BF16),
            pltpu.VMEM((S, D), BF16),
            pltpu.VMEM((D, S), BF16),
            pltpu.VMEM((D, S), BF16),
            pltpu.VMEM((D, 2 * W), BF16),
            pltpu.VMEM((D, 2 * W), BF16),
            pltpu.VMEM((S, 2 * HS), BF16),
            pltpu.VMEM((6, S, W), BF16),
            pltpu.SemaphoreType.DMA((4,)),
            pltpu.SemaphoreType.DMA((3, D // STEP)),
            pltpu.SemaphoreType.DMA((D // STEP,)),
        ],
    )(normed, cot, normed_t, cot_t, weights, kv_own)

    terms = lax.psum_scatter(terms, "y", scatter_dimension=0, tiled=True)
    mine = lax.axis_index("zh")

    def ahead(d):
        return lax.dynamic_slice_in_dim(terms, lax.rem(mine + d, ZH) * B, B, 0)

    brought = [
        lax.ppermute(ahead(d), "zh", [(i, (i + d) % ZH) for i in range(ZH)]) for d in (2, 1, 3)
    ]
    wq_grad, wo_grad = call(add_up, [arr(B, W), arr(W, B)], 4)(ahead(0), *brought)

    streams = pl.BlockSpec((NT, S, W), lambda i: (0, 0, 0))
    attn_partial, send = call(
        project,
        [arr(1, S, D), arr(NT, 3 * S + EXTRA, W)],
        56,
        flops=4 * S * D * W,
        grid=(1,),
        in_specs=[VMEM] * 2 + [streams] + [VMEM] * 2,
        out_specs=[VMEM, VMEM],
    )(kept, weights, got, gain, out_slice)
    got = lax.all_to_all(send, TENSOR, 0, 0, tiled=True)
    stream_out, stream_grad, kv_grad = call(
        finish, [arr(S, D), arr(S, W), arr(*keys_values.shape)], 12
    )(got, stream_in, cot_stream, gain_own, inv)
    return (stream_out, attn_partial, stream_grad, kv_grad, wq_grad, wo_grad)


def solution(mesh):
    fine = Mesh(mesh.devices.reshape(ZH, Y, ZL, X, CORE), FSDP + TENSOR)
    return jax.shard_map(
        per_device,
        mesh=fine,
        in_specs=(
            P(FSDP, TENSOR),
            P(TENSOR, FSDP, None),
            P(),
            P(FSDP, TENSOR),
            P(FSDP, None),
            P(TENSOR, FSDP),
            P(FSDP, TENSOR),
            P(FSDP, TENSOR),
        ),
        out_specs=(
            P(FSDP, None),
            P(TENSOR, FSDP, None),
            P(FSDP, TENSOR),
            P(FSDP, None),
            P(FSDP, TENSOR),
            P(TENSOR, FSDP),
        ),
        check_vma=False,
    )
```
